512 devices in a mesh: gz: 32 (over x, z_lo, core), gy: 16 (over z_hi, y).
Axes of the slice: x: 4, y: 4, z: 16 (z_hi: 4, z_lo: 4; z = z_hi * 4 + z_lo), core: 2. Of those that a mesh axis runs over, the one named last changes fastest.
Arguments:
- features: bfloat16 [32, 128, 128, 256], P(None, 'gz', 'gy'), may hold values from -6 to 6
- scale_first: float32 [32], replicated, may hold values from 0.5 to 2
- shift_first: float32 [32], replicated, may hold values from -3 to 3
- conv_first: bfloat16 [3, 3, 32, 32], replicated, may hold values from -0.375 to 0.375
- bias_first: float32 [32], replicated, may hold values from -3 to 3
- scale_second: float32 [32], replicated, may hold values from 0.5 to 2
- shift_second: float32 [32], replicated, may hold values from -3 to 3
- conv_second: bfloat16 [3, 3, 32, 32], replicated, may hold values from -0.375 to 0.375
- bias_second: float32 [32], replicated, may hold values from -3 to 3
- flow_weight: bfloat16 [2, 32], replicated, may hold values from -1 to 1
Outputs:
- smoothed: float32 [3, 128, 128, 256], P(None, 'gz', 'gy')
The draws below stay inside these ranges and needn't reach their ends.
All inputs are finite; a program needn't handle non-finite values.
Results may differ from the reference program's by a relative error of at most 0.0015.
Values may be sent and summed in bfloat16 or wider, within the bound.
A program may use at most 64 MiB of HBM per device.

```python
import math
import jax
import jax.numpy as jnp
from jax import lax

C = 32
NX = 256
NZ = 128
NY = 128


def block_scale(rng, dims, shards, least, largest):
    loudness = 1.0
    for position, blocks in shards:
        steps = jax.random.uniform(jax.random.fold_in(jax.random.fold_in(rng, 6), position), (blocks,), jnp.float32, least / len(shards), largest / len(shards))
        loudness = loudness * jnp.repeat(jnp.exp(steps), dims[position] // blocks).reshape((-1,) + (1,) * (len(dims) - 1 - position))
    return loudness


def normal_values(rng, shape, spread, limit, split=(), kind=jnp.bfloat16):
    drawn = spread * jax.random.normal(rng, shape, jnp.float32)
    if split:
        drawn = drawn * block_scale(rng, shape, split, -0.22, 0.18)
    return jnp.clip(drawn, -limit, limit).astype(kind)


def setup_inputs(seed: int = 0) -> dict:
    key_of = jax.random.split(jax.random.key(seed), 11)
    features = normal_values(key_of[0], (C, NZ, NY, NX), 1.0, 6.0, ((1, 32), (2, 16)))
    scale_first = jnp.clip(jnp.exp(jax.random.uniform(key_of[1], (C,), jnp.float32, math.log(0.5), math.log(2.0))), 0.5, 2.0)
    shift_first = normal_values(key_of[2], (C,), 0.5, 3.0, (), jnp.float32)
    conv_first = normal_values(key_of[3], (3, 3, C, C), (9 * C) ** -0.5, 0.375)
    bias_first = normal_values(key_of[4], (C,), 0.5, 3.0, (), jnp.float32)
    scale_second = jnp.clip(jnp.exp(jax.random.uniform(key_of[5], (C,), jnp.float32, math.log(0.5), math.log(2.0))), 0.5, 2.0)
    shift_second = normal_values(key_of[6], (C,), 0.5, 3.0, (), jnp.float32)
    conv_second = normal_values(key_of[7], (3, 3, C, C), (9 * C) ** -0.5, 0.375)
    bias_second = normal_values(key_of[8], (C,), 0.5, 3.0, (), jnp.float32)
    flow_weight = normal_values(key_of[9], (2, C), C ** -0.5, 1.0)
    return {"features": features, "scale_first": scale_first, "shift_first": shift_first, "conv_first": conv_first, "bias_first": bias_first, "scale_second": scale_second, "shift_second": shift_second, "conv_second": conv_second, "bias_second": bias_second, "flow_weight": flow_weight}


def shift_cols(source, delta):
    if delta == 0:
        return source
    zeros = jnp.zeros(source.shape[:-1] + (1,), source.dtype)
    if delta == 1:
        return jnp.concatenate([source[..., 1:], zeros], -1)
    return jnp.concatenate([zeros, source[..., :-1]], -1)


def plane_conv(source, weight, plane_axes, count_z, count_y, start_z, start_y):
    summed = None
    for row_tap in range(3):
        for col_tap in range(3):
            offset = {1: 0, 2: 0, 3: 0}
            offset[plane_axes[0]] = row_tap - 1
            offset[plane_axes[1]] = col_tap - 1
            low_z = start_z + offset[1]
            low_y = start_y + offset[2]
            window = lax.slice(source, (0, low_z, low_y, 0), (source.shape[0], low_z + count_z, low_y + count_y, source.shape[3]))
            window = shift_cols(window, offset[3])
            term = jnp.einsum('oc,czyx->ozyx', weight[row_tap, col_tap].astype(jnp.float32), window.astype(jnp.float32), preferred_element_type=jnp.float32)
            summed = term if summed is None else summed + term
    return summed


def column(vector):
    return vector[:, None, None, None]


def reference(features, scale_first, shift_first, conv_first, bias_first, scale_second, shift_second, conv_second, bias_second, flow_weight):
    depth, rows = features.shape[1], features.shape[2]
    unit = jax.nn.relu(features.astype(jnp.float32) * column(scale_first) + column(shift_first)).astype(jnp.bfloat16)
    padded = jnp.pad(unit, ((0, 0), (1, 1), (1, 1), (0, 0)))
    flows = []
    for plane_axes in ((2, 3), (1, 3), (1, 2)):
        hidden = plane_conv(padded, conv_first, plane_axes, depth, rows, 1, 1) + column(bias_first)
        active = jax.nn.relu(hidden * column(scale_second) + column(shift_second)).astype(jnp.bfloat16)
        active = jnp.pad(active, ((0, 0), (1, 1), (1, 1), (0, 0)))
        output = plane_conv(active, conv_second, plane_axes, depth, rows, 1, 1)
        block = (output + column(bias_second) + features.astype(jnp.float32)).astype(jnp.bfloat16)
        flows.append(jnp.einsum('kc,czyx->kzyx', flow_weight.astype(jnp.float32), block.astype(jnp.float32), preferred_element_type=jnp.float32))
    flow_xy, flow_xz, flow_yz = flows
    mean_flow = jnp.stack([0.5 * (flow_xz[0] + flow_yz[0]), 0.5 * (flow_xy[0] + flow_yz[1]), 0.5 * (flow_xy[1] + flow_xz[1])])
    ext = jnp.pad(mean_flow, ((0, 0), (1, 1), (1, 1), (0, 0)))
    ext = 0.25 * ext[:, :-2] + 0.5 * ext[:, 1:-1] + 0.25 * ext[:, 2:]
    ext = 0.25 * ext[:, :, :-2] + 0.5 * ext[:, :, 1:-1] + 0.25 * ext[:, :, 2:]
    return 0.25 * shift_cols(ext, -1) + 0.5 * ext + 0.25 * shift_cols(ext, 1)
```

```python
import jax
import jax.numpy as jnp
from jax import lax
from jax.experimental import pallas as pl
from jax.experimental.pallas import tpu as pltpu
from jax.sharding import PartitionSpec as P

MESH = pl.DeviceIdType.MESH
F32 = jnp.float32
BF16 = jnp.bfloat16
C = 32
Z = 4
Y = 8
X = 256
R = C * Y


def iota(shape, dim):
    return lax.broadcasted_iota(jnp.int32, shape, dim)


def dot(a, b):
    return jnp.dot(a, b, preferred_element_type=F32)


def one_hot(flags):
    return jnp.where(flags, 1.0, 0.0).astype(BF16)


def from_left(value):
    moved = pltpu.roll(value, 1, axis=1)
    return jnp.where(iota(value.shape, 1) == 0, 0.0, moved)


def from_right(value):
    last = value.shape[1] - 1
    moved = pltpu.roll(value, last, axis=1)
    return jnp.where(iota(value.shape, 1) == last, 0.0, moved)


def kernel(
    x_hbm, s1_hbm, t1_hbm, w1_hbm, b1_hbm, s2_hbm, t2_hbm, w2_hbm, b2_hbm, fw_hbm,
    out,
    xin, par, w1, w2, fw, raw, ux, edge, ez, halo,
    cols, wxy, wxz, wyz, whx, why, bxy, bxz, byz, fres, hid, acc, sm,
    rz, ys, yr,
    lsem, ssem, rsem,
):
    gz, gy = lax.axis_index("gz"), lax.axis_index("gy")
    nz, ny = lax.axis_size("gz"), lax.axis_size("gy")
    has_z = (gz > 0, gz < nz - 1)
    has_y = (gy > 0, gy < ny - 1)
    z_of = (gz - 1, gz + 1)
    y_of = (gy - 1, gy + 1)

    barrier = pltpu.get_barrier_semaphore()
    for side in range(2):
        @pl.when(has_z[side])
        def _():
            pl.semaphore_signal(barrier, inc=1, device_id=(z_of[side], gy), device_id_type=MESH)

        @pl.when(has_y[side])
        def _():
            pl.semaphore_signal(barrier, inc=1, device_id=(gz, y_of[side]), device_id_type=MESH)

    order = (0, 3, 1, 2)
    loads = {z: pltpu.make_async_copy(x_hbm.at[:, z], xin.at[:, z], lsem.at[z]) for z in order}
    params = [
        pltpu.make_async_copy(source, par.at[i], lsem.at[Z + i])
        for i, source in enumerate((s1_hbm, t1_hbm, b1_hbm, s2_hbm, t2_hbm, b2_hbm))
    ]
    weights = [
        pltpu.make_async_copy(source, target, lsem.at[Z + 6 + i])
        for i, (source, target) in enumerate(((w1_hbm, w1), (w2_hbm, w2), (fw_hbm, fw)))
    ]
    for copy in (*params, loads[0], loads[3], loads[1], loads[2], *weights):
        copy.start()

    for side in range(2):
        slot = (0, Z + 1)[side]

        @pl.when(jnp.logical_not(has_z[side]))
        def _():
            ux[slot, 1] = jnp.zeros((R, X), BF16)
            halo[slot] = jnp.zeros((2, C, X), BF16)

        @pl.when(jnp.logical_not(has_y[side]))
        def _():
            for ze in range(1, Z + 1):
                halo[ze, side] = jnp.zeros((C, X), BF16)

        for yside in range(2):
            @pl.when(has_z[side] & jnp.logical_not(has_y[yside]))
            def _():
                halo[slot, yside] = jnp.zeros((C, X), BF16)

    for copy in params:
        copy.wait()
    pick = iota((R, C), 0) // Y == iota((R, C), 1)

    def column(row):
        return jnp.sum(jnp.where(pick, row, 0.0), axis=1, keepdims=True)

    b1_row, s2_row, t2_row, b2_row = par[2], par[3], par[4], par[5]
    cols[0] = jnp.broadcast_to(column(par[0]), (R, 128))
    cols[1] = jnp.broadcast_to(column(par[1]), (R, 128))
    cols[2] = jnp.broadcast_to(column(s2_row), (R, 128))
    cols[3] = jnp.broadcast_to(column(b1_row * s2_row + t2_row), (R, 128))

    def wide(i):
        half = cols[i]
        return jnp.concatenate([half, half], axis=1)

    rows, lanes = iota((2 * C, R), 0), iota((2 * C, R), 1)
    edge_pick = one_hot(lanes == (rows % C) * Y + (rows // C) * (Y - 1))
    for z in order:
        loads[z].wait()
        value = xin[:, z].astype(F32).reshape(R, X)
        raw[z] = value.astype(BF16)
        unit = jnp.maximum(value * wide(0) + wide(1), 0.0).astype(BF16)
        ux[z + 1, 1] = unit
        edge[z] = dot(edge_pick, unit).astype(BF16).reshape(2, C, X)

    def remote(source, target, i, zi, yi):
        return pltpu.make_async_remote_copy(
            src_ref=source, dst_ref=target, send_sem=ssem.at[i], recv_sem=rsem.at[i],
            device_id=(zi, yi), device_id_type=MESH,
        )

    send_ez = [remote(edge.at[(0, Z - 1)[s]], ez.at[1 - s], s, z_of[s], gy) for s in range(2)]
    send_slab = [
        remote(ux.at[(1, Z)[s], 1], ux.at[(Z + 1, 0)[s], 1], 2 + s, z_of[s], gy) for s in range(2)
    ]
    send_y = [
        remote(edge.at[:, s], halo.at[pl.ds(1, Z), 1 - s], 4 + s, gz, y_of[s]) for s in range(2)
    ]
    send_corner = [
        [
            remote(ez.at[zs, ys_], halo.at[(0, Z + 1)[zs], 1 - ys_], 6 + 2 * zs + ys_, gz, y_of[ys_])
            for ys_ in range(2)
        ]
        for zs in range(2)
    ]

    peers = sum(flag.astype(jnp.int32) for flag in (*has_z, *has_y))
    pl.semaphore_wait(barrier, peers)

    for side in range(2):
        @pl.when(has_z[side])
        def _():
            send_ez[side].start()
    for side in range(2):
        @pl.when(has_y[side])
        def _():
            send_y[side].start()
    for side in range(2):
        @pl.when(has_z[side])
        def _():
            send_slab[side].start()

    for copy in weights:
        copy.wait()
    spread = one_hot(iota((C, R), 1) // Y == iota((C, R), 0))
    repeat = one_hot(pick)
    wide_w1 = dot(w1[...].reshape(9 * C, C), spread).astype(BF16)
    shift = iota((R, R), 1) % Y - iota((R, R), 0) % Y
    for j in range(3):
        banded = None
        for i in range(3):
            k = 3 * i + j
            full = dot(repeat, wide_w1[k * C : (k + 1) * C])
            term = jnp.where(shift == i - 1, full, 0.0)
            banded = term if banded is None else banded + term
            wxz[i, :, j * R : (j + 1) * R] = jnp.where(shift == 0, full, 0.0).astype(BF16)
        wxy[:, j * R : (j + 1) * R] = banded.astype(BF16)
    for i in range(3):
        banded = None
        for j in range(3):
            k = 3 * i + j
            full = dot(repeat, wide_w1[k * C : (k + 1) * C])
            term = jnp.where(shift == j - 1, full, 0.0)
            banded = term if banded is None else banded + term
        wyz[i] = banded.astype(BF16)
    reach = 6 * C
    rows, lanes = iota((R, reach), 0) % Y, (iota((R, reach), 1) // C) % 2
    touched = ((rows == 0) & (lanes == 0)) | ((rows == Y - 1) & (lanes == 1))
    packed_x = jnp.zeros((C, reach), F32)
    packed_y = jnp.zeros((C, reach), F32)
    for tap in range(3):
        for side in range(2):
            put = one_hot(iota((C, reach), 1) == iota((C, reach), 0) + (2 * tap + side) * C)
            packed_x += dot(w1[2 * side, tap], put)
            packed_y += dot(w1[tap, 2 * side], put)
    whx[...] = jnp.where(touched, dot(repeat, packed_x.astype(BF16)), 0.0).astype(BF16)
    why[...] = jnp.where(touched, dot(repeat, packed_y.astype(BF16)), 0.0).astype(BF16)

    lanes16 = iota((16, R), 1) % Y
    rows16 = iota((16, R), 0)
    fw16 = jnp.where(
        iota((16, C), 0) < Y, jnp.broadcast_to(fw[0:1, :].astype(F32), (16, C)),
        jnp.broadcast_to(fw[1:2, :].astype(F32), (16, C)),
    )
    fres[...] = jnp.where(rows16 % Y == lanes16, dot(fw16.astype(BF16), spread), 0.0).astype(BF16)
    bias = jnp.sum(fw16 * b2_row, axis=1, keepdims=True)
    for k in range(2):
        fw_k = jnp.broadcast_to(fw[k : k + 1, :].astype(F32), (16, C)).astype(BF16)
        taps = {}
        for i in range(3):
            for j in range(3):
                g = dot(fw_k, w2[i, j])
                high = g.astype(BF16)
                low = (g - high.astype(F32)).astype(BF16)
                taps[i, j] = (dot(high, spread), dot(low, spread))
        for part in range(2):
            for a in range(3):
                band_xy = jnp.zeros((16, R), F32)
                band_yz = jnp.zeros((16, R), F32)
                for b in range(3):
                    hit = rows16 == (lanes16 + (17 - b)) % 16
                    band_xy += jnp.where(hit, taps[b, a][part], 0.0)
                    band_yz += jnp.where(hit, taps[a, b][part], 0.0)
                at = ((part * 3 + a) * 2 + k) * 16
                bxy[at : at + 16, :] = band_xy.astype(BF16)
                byz[at : at + 16, :] = band_yz.astype(BF16)
        for i in range(3):
            for j in range(3):
                for part in range(2):
                    at = ((part * 9 + i * 3 + j) * 2) * Y
                    keep = (rows16 // Y == k) & (rows16 % Y == lanes16)
                    value = jnp.where(keep, taps[i, j][part], 0.0)
                    if k == 0:
                        bxz[at : at + 16, :] = value.astype(BF16)
                    else:
                        bxz[at : at + 16, :] = (bxz[at : at + 16, :].astype(F32) + value).astype(BF16)

    def shifted(ze):
        value = ux[ze, 1].astype(F32)
        ux[ze, 0] = from_left(value).astype(BF16)
        ux[ze, 2] = from_right(value).astype(BF16)

    for ze in range(1, Z + 1):
        shifted(ze)

    for side in range(2):
        @pl.when(has_z[side])
        def _():
            send_ez[side].wait_send()
            send_ez[1 - side].wait_recv()
            for yside in range(2):
                @pl.when(has_y[yside])
                def _():
                    send_corner[side][yside].start()

    acc[...] = jnp.zeros_like(acc)
    for z in range(Z):
        hid[0, z] = dot(wxy[...], ux[z + 1].reshape(3 * R, X))
        xz = dot(wxz[1], ux[z + 1].reshape(3 * R, X))
        yz = dot(wyz[1], ux[z + 1, 1])
        for i in (0, 2):
            if 1 <= z + i <= Z:
                xz += dot(wxz[i], ux[z + i].reshape(3 * R, X))
                yz += dot(wyz[i], ux[z + i, 1])
        hid[1, z] = xz
        hid[2, z] = yz
        residual = dot(fres[...], raw[z]) + bias
        r0, r1 = residual[:Y], residual[Y:]
        acc[1, z + 1, 0, 0] = 2.0 * r0
        acc[1, z + 1, 1, 0] = r0 + r1
        acc[1, z + 1, 2, 0] = 2.0 * r1

    for side in range(2):
        @pl.when(has_z[side])
        def _():
            send_slab[1 - side].wait_recv()
    for ze in (0, Z + 1):
        shifted(ze)
    for z, i in ((0, 0), (Z - 1, 2)):
        hid[1, z] += dot(wxz[i], ux[z + i].reshape(3 * R, X))
        hid[2, z] += dot(wyz[i], ux[z + i, 1])

    def active(plane, z):
        return jnp.maximum(hid[plane, z] * wide(2) + wide(3), 0.0).astype(BF16)

    for z in range(Z):
        both = dot(bxz[...], active(1, z))
        part = both[:144] + both[144:]
        for i in range(3):
            for j in range(3):
                at = (i * 3 + j) * 16
                acc[j, z + 2 - i, 0, 0] += part[at : at + Y]
                acc[j, z + 2 - i, 2, 0] += part[at + Y : at + 16]

    for side in range(2):
        @pl.when(has_y[side])
        def _():
            send_y[1 - side].wait_recv()
            for zside in range(2):
                @pl.when(has_z[zside])
                def _():
                    send_corner[zside][1 - side].wait_recv()
    for z in range(Z):
        beside = halo[z + 1].reshape(2 * C, X)
        wider = beside.astype(F32)
        three = jnp.concatenate([from_left(wider).astype(BF16), beside, from_right(wider).astype(BF16)], axis=0)
        hid[0, z] += dot(whx[...], three)
        hid[2, z] += dot(why[...], halo[z : z + 3].reshape(6 * C, X))
        both = dot(bxy[...], active(0, z))
        part = (both[:96] + both[96:]).reshape(3, 2, 2, Y, X)
        for j in range(3):
            acc[j, z + 1, 1] += part[j, 0]
            acc[j, z + 1, 2] += part[j, 1]
        both = dot(byz[...], active(2, z))
        part = (both[:96] + both[96:]).reshape(3, 2, 2, Y, X)
        for i in range(3):
            acc[1, z + 2 - i, 0] += part[i, 0]
            acc[1, z + 2 - i, 1] += part[i, 1]

    rows16x = iota((16, X), 0)
    outside = ((rows16x == 15) & jnp.logical_not(has_y[0])) | ((rows16x == Y) & jnp.logical_not(has_y[1]))
    flow = {}
    for ze in range(Z + 2):
        for comp in range(3):
            value = (
                from_left(acc[0, ze, comp].reshape(16, X))
                + acc[1, ze, comp].reshape(16, X)
                + from_right(acc[2, ze, comp].reshape(16, X))
            )
            value = jnp.where(outside, 0.0, value)
            if ze == 0:
                value = jnp.where(has_z[0], value, 0.0)
            if ze == Z + 1:
                value = jnp.where(has_z[1], value, 0.0)
            value = 0.125 * (from_left(value) + from_right(value)) + 0.25 * value
            flow[ze, comp] = 0.5 * value + 0.25 * (pltpu.roll(value, 1, axis=0) + pltpu.roll(value, 15, axis=0))
    for comp in range(3):
        for zs in range(Z + 4):
            value = None
            for ze, weight in ((zs - 2, 0.25), (zs - 1, 0.5), (zs, 0.25)):
                if 0 <= ze < Z + 2:
                    term = weight * flow[ze, comp]
                    value = term if value is None else value + term
            sm[0, zs, comp] = value[:Y]
            sm[1, zs, comp] = value[Y:]

    send_rz = [
        [
            remote(sm.at[t, pl.ds((0, Z + 2)[s], 2)], rz.at[1 - s, t], 10 + 2 * t + s, z_of[s], gy)
            for s in range(2)
        ]
        for t in range(2)
    ]
    send_ry = [remote(ys.at[s], yr.at[1 - s], 14 + s, gz, y_of[s]) for s in range(2)]
    for t in (1, 0):
        for side in range(2):
            @pl.when(has_z[side])
            def _():
                send_rz[t][side].start()
    for side in range(2):
        @pl.when(jnp.logical_not(has_z[side]))
        def _():
            rz[side] = jnp.zeros((2, 2, 3, Y, X), F32)

        @pl.when(jnp.logical_not(has_y[side]))
        def _():
            yr[side] = jnp.zeros((3, Y, X), F32)

    for side in range(2):
        @pl.when(has_z[side])
        def _():
            send_rz[1][1 - side].wait_recv()
    row = iota((Y, X), 0)
    for comp in range(3):
        up, down = None, None
        for z in range(Z):
            value = sm[1, z + 2, comp] + rz[z // 2, 1, z % 2, comp]
            high = jnp.where(row < 2, value, 0.0)
            low = jnp.where(row >= Y - 2, value, 0.0)
            if z:
                high = pltpu.roll(high, 2 * z, axis=0)
            if z < Z - 1:
                low = pltpu.roll(low, 2 * z + 2, axis=0)
            up = high if up is None else up + high
            down = low if down is None else down + low
        ys[1, comp] = up
        ys[0, comp] = down
    for side in range(2):
        @pl.when(has_y[side])
        def _():
            send_ry[side].start()
    for side in range(2):
        @pl.when(has_z[side])
        def _():
            send_rz[0][1 - side].wait_recv()
    for comp in range(3):
        for z in range(Z):
            sm[0, z + 2, comp] += rz[z // 2, 0, z % 2, comp]
    for side in range(2):
        @pl.when(has_y[side])
        def _():
            send_ry[1 - side].wait_recv()
    for comp in range(3):
        for z in range(Z):
            first = yr[0, comp]
            if z:
                first = pltpu.roll(first, Y - 2 * z, axis=0)
            last = yr[1, comp]
            if z < Z - 1:
                last = pltpu.roll(last, Y - 2 - 2 * z, axis=0)
            beyond = jnp.where(row < 2, first, jnp.where(row >= Y - 2, last, 0.0))
            out[comp, z] = sm[0, z + 2, comp] + beyond

    for side in range(2):
        @pl.when(has_z[side])
        def _():
            send_slab[side].wait_send()
            send_rz[0][side].wait_send()
            send_rz[1][side].wait_send()

        @pl.when(has_y[side])
        def _():
            send_y[side].wait_send()
            send_ry[side].wait_send()
            for zside in range(2):
                @pl.when(has_z[zside])
                def _():
                    send_corner[zside][side].wait_send()


def block(features, s1, t1, w1, b1, s2, t2, w2, b2, fw):
    def row(v):
        return v.reshape(1, C)

    vm = pltpu.VMEM
    dma = pltpu.SemaphoreType.DMA
    return pl.pallas_call(
        kernel,
        out_shape=jax.ShapeDtypeStruct((3, Z, Y, X), F32),
        in_specs=[pl.BlockSpec(memory_space=pl.ANY)] * 10,
        out_specs=pl.BlockSpec(memory_space=pltpu.VMEM),
        scratch_shapes=[
            vm((C, Z, Y, X), BF16),
            vm((6, 1, C), F32),
            vm((3, 3, C, C), BF16),
            vm((3, 3, C, C), BF16),
            vm((2, C), BF16),
            vm((Z, R, X), BF16),
            vm((Z + 2, 3, R, X), BF16),
            vm((Z, 2, C, X), BF16),
            vm((2, 2, C, X), BF16),
            vm((Z + 2, 2, C, X), BF16),
            vm((4, R, 128), F32),
            vm((R, 3 * R), BF16),
            vm((3, R, 3 * R), BF16),
            vm((3, R, R), BF16),
            vm((R, 6 * C), BF16),
            vm((R, 6 * C), BF16),
            vm((192, R), BF16),
            vm((288, R), BF16),
            vm((192, R), BF16),
            vm((16, R), BF16),
            vm((3, Z, R, X), F32),
            vm((3, Z + 2, 3, 2, Y, X), F32),
            vm((2, Z + 4, 3, Y, X), F32),
            vm((2, 2, 2, 3, Y, X), F32),
            vm((2, 3, Y, X), F32),
            vm((2, 3, Y, X), F32),
            dma((Z + 9,)),
            dma((16,)),
            dma((16,)),
        ],
        compiler_params=pltpu.CompilerParams(
            collective_id=0, has_side_effects=True, vmem_limit_bytes=48 * 1024 * 1024
        ),
    )(features, row(s1), row(t1), w1, row(b1), row(s2), row(t2), w2, row(b2), fw)


def solution(mesh):
    return jax.shard_map(
        block,
        mesh=mesh,
        in_specs=(P(None, "gz", "gy", None), P(), P(), P(), P(), P(), P(), P(), P(), P()),
        out_specs=P(None, "gz", "gy", None),
        check_vma=False,
    )
```

```python
import jax
import jax.numpy as jnp
from jax import lax
from jax.experimental import pallas as pl
from jax.experimental.pallas import tpu as pltpu
from jax.sharding import PartitionSpec as P

MESH = pl.DeviceIdType.MESH
F32 = jnp.float32
BF16 = jnp.bfloat16
C = 32
Z = 4
Y = 8
X = 256
R = C * Y


def iota(shape, dim):
    return lax.broadcasted_iota(jnp.int32, shape, dim)


def dot(a, b):
    return jnp.dot(a, b, preferred_element_type=F32)


def one_hot(flags):
    return jnp.where(flags, 1.0, 0.0).astype(BF16)


def from_left(value):
    moved = pltpu.roll(value, 1, axis=1)
    return jnp.where(iota(value.shape, 1) == 0, 0.0, moved)


def from_right(value):
    last = value.shape[1] - 1
    moved = pltpu.roll(value, last, axis=1)
    return jnp.where(iota(value.shape, 1) == last, 0.0, moved)


def kernel(
    x_hbm, s1_hbm, t1_hbm, w1_hbm, b1_hbm, s2_hbm, t2_hbm, w2_hbm, b2_hbm, fw_hbm,
    out,
    xin, par, w1, w2, fw, raw, ux, edge, ez, halo,
    cols, cols_e, wxy, wxz, wyz, wxy_e, wyz_e, whx, why, bxy, bxz, byz, bxy_e, byz_e, fres,
    hid, hid_e, acc, sm,
    rz, ys, yr, ds, dr,
    lsem, ssem, rsem,
):
    gz, gy = lax.axis_index("gz"), lax.axis_index("gy")
    nz, ny = lax.axis_size("gz"), lax.axis_size("gy")
    has_z = (gz > 0, gz < nz - 1)
    has_y = (gy > 0, gy < ny - 1)
    z_of = (gz - 1, gz + 1)
    y_of = (gy - 1, gy + 1)

    barrier = pltpu.get_barrier_semaphore()
    for side in range(2):
        @pl.when(has_z[side])
        def _():
            pl.semaphore_signal(barrier, inc=1, device_id=(z_of[side], gy), device_id_type=MESH)

        @pl.when(has_y[side])
        def _():
            pl.semaphore_signal(barrier, inc=1, device_id=(gz, y_of[side]), device_id_type=MESH)

    order = (0, 3, 1, 2)
    loads = {z: pltpu.make_async_copy(x_hbm.at[:, z], xin.at[:, z], lsem.at[z]) for z in order}
    params = [
        pltpu.make_async_copy(source, par.at[i], lsem.at[Z + i])
        for i, source in enumerate((s1_hbm, t1_hbm, b1_hbm, s2_hbm, t2_hbm, b2_hbm))
    ]
    weights = [
        pltpu.make_async_copy(source, target, lsem.at[Z + 6 + i])
        for i, (source, target) in enumerate(((w1_hbm, w1), (w2_hbm, w2), (fw_hbm, fw)))
    ]
    for copy in (*params, loads[0], loads[3], loads[1], loads[2], *weights):
        copy.start()

    for side in range(2):
        slot = (0, Z + 1)[side]

        @pl.when(jnp.logical_not(has_z[side]))
        def _():
            ux[slot, 1] = jnp.zeros((R, X), BF16)
            halo[slot] = jnp.zeros((2, C, X), BF16)

        @pl.when(jnp.logical_not(has_y[side]))
        def _():
            for ze in range(1, Z + 1):
                halo[ze, side] = jnp.zeros((C, X), BF16)

        for yside in range(2):
            @pl.when(has_z[side] & jnp.logical_not(has_y[yside]))
            def _():
                halo[slot, yside] = jnp.zeros((C, X), BF16)

    for copy in params:
        copy.wait()
    pick = iota((R, C), 0) // Y == iota((R, C), 1)

    def column(row):
        return jnp.sum(jnp.where(pick, row, 0.0), axis=1, keepdims=True)

    b1_row, s2_row, t2_row, b2_row = par[2], par[3], par[4], par[5]
    cols[0] = jnp.broadcast_to(column(par[0]), (R, 128))
    cols[1] = jnp.broadcast_to(column(par[1]), (R, 128))
    cols[2] = jnp.broadcast_to(column(s2_row), (R, 128))
    cols[3] = jnp.broadcast_to(column(b1_row * s2_row + t2_row), (R, 128))

    pick_e = iota((2 * C, C), 0) % C == iota((2 * C, C), 1)
    cols_e[0] = jnp.broadcast_to(
        jnp.sum(jnp.where(pick_e, s2_row, 0.0), axis=1, keepdims=True), (2 * C, 128)
    )
    cols_e[1] = jnp.broadcast_to(
        jnp.sum(jnp.where(pick_e, b1_row * s2_row + t2_row, 0.0), axis=1, keepdims=True), (2 * C, 128)
    )

    def wide(half):
        return jnp.concatenate([half, half], axis=1)

    rows, lanes = iota((2 * C, R), 0), iota((2 * C, R), 1)
    edge_pick = one_hot(lanes == (rows % C) * Y + (rows // C) * (Y - 1))
    for z in order:
        loads[z].wait()
        value = xin[:, z].astype(F32).reshape(R, X)
        raw[z] = value.astype(BF16)
        unit = jnp.maximum(value * wide(cols[0]) + wide(cols[1]), 0.0).astype(BF16)
        ux[z + 1, 1] = unit
        edge[z] = dot(edge_pick, unit).astype(BF16).reshape(2, C, X)

    def remote(source, target, i, zi, yi):
        return pltpu.make_async_remote_copy(
            src_ref=source, dst_ref=target, send_sem=ssem.at[i], recv_sem=rsem.at[i],
            device_id=(zi, yi), device_id_type=MESH,
        )

    send_ez = [remote(edge.at[(0, Z - 1)[s]], ez.at[1 - s], s, z_of[s], gy) for s in range(2)]
    send_slab = [
        remote(ux.at[(1, Z)[s], 1], ux.at[(Z + 1, 0)[s], 1], 2 + s, z_of[s], gy) for s in range(2)
    ]
    send_y = [
        remote(edge.at[:, s], halo.at[pl.ds(1, Z), 1 - s], 4 + s, gz, y_of[s]) for s in range(2)
    ]
    send_corner = [
        [
            remote(ez.at[zs, ys_], halo.at[(0, Z + 1)[zs], 1 - ys_], 6 + 2 * zs + ys_, gz, y_of[ys_])
            for ys_ in range(2)
        ]
        for zs in range(2)
    ]

    for copy in weights:
        copy.wait()
    spread = one_hot(iota((C, R), 1) // Y == iota((C, R), 0))
    repeat = one_hot(pick)
    wide_w1 = dot(w1[...].reshape(9 * C, C), spread).astype(BF16)
    shift = iota((R, R), 1) % Y - iota((R, R), 0) % Y
    for j in range(3):
        banded = None
        for i in range(3):
            k = 3 * i + j
            full = dot(repeat, wide_w1[k * C : (k + 1) * C])
            term = jnp.where(shift == i - 1, full, 0.0)
            banded = term if banded is None else banded + term
            wxz[i, :, j * R : (j + 1) * R] = jnp.where(shift == 0, full, 0.0).astype(BF16)
        wxy[:, j * R : (j + 1) * R] = banded.astype(BF16)
    for i in range(3):
        banded = None
        for j in range(3):
            k = 3 * i + j
            full = dot(repeat, wide_w1[k * C : (k + 1) * C])
            term = jnp.where(shift == j - 1, full, 0.0)
            banded = term if banded is None else banded + term
        wyz[i] = banded.astype(BF16)
    for i in range(3):
        wyz_e[i] = dot(edge_pick, wyz[i]).astype(BF16)
    wxy_e[...] = dot(edge_pick, wxy[...]).astype(BF16)
    reach = 6 * C
    touched = iota((2 * C, reach), 0) // C == (iota((2 * C, reach), 1) // C) % 2
    repeat_e = one_hot(pick_e)
    packed_x = jnp.zeros((C, reach), F32)
    packed_y = jnp.zeros((C, reach), F32)
    for tap in range(3):
        for side in range(2):
            put = one_hot(iota((C, reach), 1) == iota((C, reach), 0) + (2 * tap + side) * C)
            packed_x += dot(w1[2 * side, tap], put)
            packed_y += dot(w1[tap, 2 * side], put)
    whx[...] = jnp.where(touched, dot(repeat_e, packed_x.astype(BF16)), 0.0).astype(BF16)
    why[...] = jnp.where(touched, dot(repeat_e, packed_y.astype(BF16)), 0.0).astype(BF16)

    rows, lanes = iota((2 * 16, R), 0) % 16, iota((2 * 16, R), 1) % Y
    first = jnp.broadcast_to(fw[0:1, :].astype(F32), (16, C))
    second = jnp.broadcast_to(fw[1:2, :].astype(F32), (16, C))
    fw32 = jnp.concatenate([first, second], axis=0)
    fw16 = jnp.concatenate([first[:Y], second[:Y]], axis=0)
    highs, lows = [], []
    for i in range(3):
        for j in range(3):
            g = dot(fw32.astype(BF16), w2[i, j])
            high = g.astype(BF16)
            highs.append(high)
            lows.append((g - high.astype(F32)).astype(BF16))
    taps = dot(jnp.concatenate(highs + lows, axis=0), spread).reshape(2, 3, 3, 32, R)
    same = rows == lanes
    for part in range(2):
        for a in range(3):
            band_xy = jnp.zeros((32, R), F32)
            band_yz = jnp.zeros((32, R), F32)
            for b in range(3):
                hit = rows == (lanes + (17 - b)) % 16
                band_xy += jnp.where(hit, taps[part, b, a], 0.0)
                band_yz += jnp.where(hit, taps[part, a, b], 0.0)
            at = (part * 3 + a) * 32
            bxy[at : at + 32, :] = band_xy.astype(BF16)
            byz[at : at + 32, :] = band_yz.astype(BF16)
        for i in range(3):
            for j in range(3):
                value = jnp.where(same, taps[part, i, j], 0.0)
                at = (part * 9 + i * 3 + j) * 16
                bxz[at : at + 16, :] = jnp.concatenate([value[:Y], value[16 : 16 + Y]], axis=0).astype(BF16)
    rows, lanes = iota((R, 2 * C), 0), iota((R, 2 * C), 1)
    edge_put = one_hot(rows == (lanes % C) * Y + (lanes // C) * (Y - 1))
    bxy_e[...] = dot(bxy[...], edge_put).astype(BF16)
    byz_e[...] = dot(byz[...], edge_put).astype(BF16)
    own = iota((16, R), 0) % Y == iota((16, R), 1) % Y
    fres[...] = jnp.where(own, dot(fw16.astype(BF16), spread), 0.0).astype(BF16)
    bias = jnp.sum(fw16 * b2_row, axis=1, keepdims=True)

    peers = sum(flag.astype(jnp.int32) for flag in (*has_z, *has_y))
    pl.semaphore_wait(barrier, peers)

    for side in range(2):
        @pl.when(has_z[side])
        def _():
            send_ez[side].start()
    for side in range(2):
        @pl.when(has_y[side])
        def _():
            send_y[side].start()
    for side in range(2):
        @pl.when(has_z[side])
        def _():
            send_slab[side].start()

    def shifted(ze):
        value = ux[ze, 1].astype(F32)
        ux[ze, 0] = from_left(value).astype(BF16)
        ux[ze, 2] = from_right(value).astype(BF16)

    for ze in range(1, Z + 1):
        shifted(ze)

    row8 = iota((R, X), 0) % Y
    inner = (row8 > 0) & (row8 < Y - 1)

    def active(hidden):
        return jnp.maximum(hidden * wide(cols[2]) + wide(cols[3]), 0.0)

    def active_e(hidden):
        return jnp.maximum(hidden * wide(cols_e[0]) + wide(cols_e[1]), 0.0).astype(BF16)

    def add_xy(z, both):
        part = (both[:96] + both[96:]).reshape(3, 2, 2, Y, X)
        for j in range(3):
            acc[j, z + 1, 1] += part[j, 0]
            acc[j, z + 1, 2] += part[j, 1]

    def add_yz(z, both):
        part = (both[:96] + both[96:]).reshape(3, 2, 2, Y, X)
        for i in range(3):
            acc[1, z + 2 - i, 0] += part[i, 0]
            acc[1, z + 2 - i, 1] += part[i, 1]

    acc[...] = jnp.zeros_like(acc)
    for z in range(Z):
        wide_x = ux[z + 1].reshape(3 * R, X)
        hid_e[0, z] = dot(wxy_e[...], wide_x)
        value = jnp.where(inner, active(dot(wxy[...], wide_x)), 0.0).astype(BF16)
        add_xy(z, dot(bxy[...], value))

    for side in range(2):
        @pl.when(has_z[side])
        def _():
            send_ez[side].wait_send()
            send_ez[1 - side].wait_recv()
            for yside in range(2):
                @pl.when(has_y[yside])
                def _():
                    send_corner[side][yside].start()

    for z in range(Z):
        xz = dot(wxz[1], ux[z + 1].reshape(3 * R, X))
        yz = dot(wyz[1], ux[z + 1, 1])
        yz_e = dot(wyz_e[1], ux[z + 1, 1])
        for i in (0, 2):
            if 1 <= z + i <= Z:
                xz += dot(wxz[i], ux[z + i].reshape(3 * R, X))
                yz += dot(wyz[i], ux[z + i, 1])
                yz_e += dot(wyz_e[i], ux[z + i, 1])
        hid[0, z] = xz
        hid[1, z] = yz
        hid_e[1, z] = yz_e
        residual = dot(fres[...], raw[z]) + bias
        r0, r1 = residual[:Y], residual[Y:]
        acc[1, z + 1, 0, 0] += 2.0 * r0
        acc[1, z + 1, 1, 0] += r0 + r1
        acc[1, z + 1, 2, 0] += 2.0 * r1

    def finish(z):
        both = dot(bxz[...], active(hid[0, z]).astype(BF16))
        part = both[:144] + both[144:]
        for i in range(3):
            for j in range(3):
                at = (i * 3 + j) * 16
                acc[j, z + 2 - i, 0, 0] += part[at : at + Y]
                acc[j, z + 2 - i, 2, 0] += part[at + Y : at + 16]
        add_yz(z, dot(byz[...], jnp.where(inner, active(hid[1, z]), 0.0).astype(BF16)))

    for z in range(1, Z - 1):
        finish(z)

    for side in range(2):
        @pl.when(has_z[side])
        def _():
            send_slab[1 - side].wait_recv()
    for ze in (0, Z + 1):
        shifted(ze)
    for z, i in ((0, 0), (Z - 1, 2)):
        hid[0, z] += dot(wxz[i], ux[z + i].reshape(3 * R, X))
        hid[1, z] += dot(wyz[i], ux[z + i, 1])
        hid_e[1, z] += dot(wyz_e[i], ux[z + i, 1])
        finish(z)

    for side in range(2):
        @pl.when(has_y[side])
        def _():
            send_y[1 - side].wait_recv()
    for z in range(Z):
        beside = halo[z + 1].reshape(2 * C, X)
        wider = beside.astype(F32)
        three = jnp.concatenate([from_left(wider).astype(BF16), beside, from_right(wider).astype(BF16)], axis=0)
        add_xy(z, dot(bxy_e[...], active_e(hid_e[0, z] + dot(whx[...], three))))
    for side in range(2):
        @pl.when(has_y[side])
        def _():
            for zside in range(2):
                @pl.when(has_z[zside])
                def _():
                    send_corner[zside][1 - side].wait_recv()
    for z in range(Z):
        hidden = hid_e[1, z] + dot(why[...], halo[z : z + 3].reshape(6 * C, X))
        add_yz(z, dot(byz_e[...], active_e(hidden)))

    rows16x = iota((16, X), 0)
    outside = ((rows16x == 15) & jnp.logical_not(has_y[0])) | ((rows16x == Y) & jnp.logical_not(has_y[1]))
    flow = {}
    for ze in range(Z + 2):
        for comp in range(3):
            value = (
                from_left(acc[0, ze, comp].reshape(16, X))
                + acc[1, ze, comp].reshape(16, X)
                + from_right(acc[2, ze, comp].reshape(16, X))
            )
            value = jnp.where(outside, 0.0, value)
            if ze == 0:
                value = jnp.where(has_z[0], value, 0.0)
            if ze == Z + 1:
                value = jnp.where(has_z[1], value, 0.0)
            value = 0.125 * (from_left(value) + from_right(value)) + 0.25 * value
            flow[ze, comp] = 0.5 * value + 0.25 * (pltpu.roll(value, 1, axis=0) + pltpu.roll(value, 15, axis=0))
    for comp in range(3):
        for zs in range(Z + 4):
            value = None
            for ze, weight in ((zs - 2, 0.25), (zs - 1, 0.5), (zs, 0.25)):
                if 0 <= ze < Z + 2:
                    term = weight * flow[ze, comp]
                    value = term if value is None else value + term
            sm[0, zs, comp] = value[:Y]
            sm[1, zs, comp] = value[Y:]

    send_rz = [remote(sm.at[0, pl.ds((0, Z + 2)[t], 2)], rz.at[1 - t], 10 + t, z_of[t], gy) for t in range(2)]
    send_ry = [remote(ys.at[s], yr.at[1 - s], 12 + s, gz, y_of[s]) for s in range(2)]
    send_rd = [
        [remote(ds.at[t, s], dr.at[1 - t, 1 - s], 14 + 2 * t + s, z_of[t], y_of[s]) for s in range(2)]
        for t in range(2)
    ]
    row = iota((Y, X), 0)
    sent = (row >= Y - 2, row < 2)

    def moved(value, by):
        return pltpu.roll(value, by % Y, axis=0) if by % Y else value

    for s in range(2):
        for t in range(2):
            for tile in range(2):
                packed = None
                for comp in range(3):
                    for q in range(2):
                        if comp // 2 == tile:
                            value = jnp.where(sent[s], sm[1, (0, Z + 2)[t] + q, comp], 0.0)
                            value = moved(value, (comp % 2) * 4 + 2 * q + (2, 0)[s])
                            packed = value if packed is None else packed + value
                ds[t, s, tile] = packed

            @pl.when(has_z[t] & has_y[s])
            def _():
                send_rd[t][s].start()
    for s in range(2):
        for comp in range(3):
            packed = None
            for z in range(Z):
                value = moved(jnp.where(sent[s], sm[1, z + 2, comp], 0.0), 2 * z + (2, 0)[s])
                packed = value if packed is None else packed + value
            ys[s, comp] = packed

        @pl.when(has_y[s])
        def _():
            send_ry[s].start()
    for t in range(2):
        @pl.when(has_z[t])
        def _():
            send_rz[t].start()

    for side in range(2):
        @pl.when(jnp.logical_not(has_z[side]))
        def _():
            rz[side] = jnp.zeros((2, 3, Y, X), F32)

        @pl.when(jnp.logical_not(has_y[side]))
        def _():
            yr[side] = jnp.zeros((3, Y, X), F32)

        for s in range(2):
            @pl.when(jnp.logical_not(has_z[side] & has_y[s]))
            def _():
                dr[side, s] = jnp.zeros((2, Y, X), F32)

    for side in range(2):
        @pl.when(has_z[side])
        def _():
            send_rz[1 - side].wait_recv()

        @pl.when(has_y[side])
        def _():
            send_ry[1 - side].wait_recv()

        for s in range(2):
            @pl.when(has_z[side] & has_y[s])
            def _():
                send_rd[1 - side][1 - s].wait_recv()
    for comp in range(3):
        for z in range(Z):
            t, q = z // 2, z % 2
            beyond = []
            for s in range(2):
                to = (0, Y - 2)[s]
                value = moved(yr[s, comp], to - 2 * z)
                value += moved(dr[t, s, comp // 2], to - (comp % 2) * 4 - 2 * q)
                beyond.append(value)
            value = jnp.where(row < 2, beyond[0], jnp.where(row >= Y - 2, beyond[1], 0.0))
            out[comp, z] = sm[0, z + 2, comp] + rz[t, q, comp] + value

    for side in range(2):
        @pl.when(has_z[side])
        def _():
            send_slab[side].wait_send()
            send_rz[side].wait_send()

        @pl.when(has_y[side])
        def _():
            send_y[side].wait_send()
            send_ry[side].wait_send()

        for s in range(2):
            @pl.when(has_z[side] & has_y[s])
            def _():
                send_corner[side][s].wait_send()
                send_rd[side][s].wait_send()


def block(features, s1, t1, w1, b1, s2, t2, w2, b2, fw):
    def row(v):
        return v.reshape(1, C)

    vm = pltpu.VMEM
    dma = pltpu.SemaphoreType.DMA
    return pl.pallas_call(
        kernel,
        out_shape=pltpu.VMEM((3, Z, Y, X), F32),
        in_specs=[pl.BlockSpec(memory_space=pltpu.HBM)] * 10,
        out_specs=pl.BlockSpec(memory_space=pltpu.VMEM),
        scratch_shapes=[
            vm((C, Z, Y, X), BF16),
            vm((6, 1, C), F32),
            vm((3, 3, C, C), BF16),
            vm((3, 3, C, C), BF16),
            vm((2, C), BF16),
            vm((Z, R, X), BF16),
            vm((Z + 2, 3, R, X), BF16),
            vm((Z, 2, C, X), BF16),
            vm((2, 2, C, X), BF16),
            vm((Z + 2, 2, C, X), BF16),
            vm((4, R, 128), F32),
            vm((2, 2 * C, 128), F32),
            vm((R, 3 * R), BF16),
            vm((3, R, 3 * R), BF16),
            vm((3, R, R), BF16),
            vm((2 * C, 3 * R), BF16),
            vm((3, 2 * C, R), BF16),
            vm((2 * C, 6 * C), BF16),
            vm((2 * C, 6 * C), BF16),
            vm((192, R), BF16),
            vm((288, R), BF16),
            vm((192, R), BF16),
            vm((192, 2 * C), BF16),
            vm((192, 2 * C), BF16),
            vm((16, R), BF16),
            vm((2, Z, R, X), F32),
            vm((2, Z, 2 * C, X), F32),
            vm((3, Z + 2, 3, 2, Y, X), F32),
            vm((2, Z + 4, 3, Y, X), F32),
            vm((2, 2, 3, Y, X), F32),
            vm((2, 3, Y, X), F32),
            vm((2, 3, Y, X), F32),
            vm((2, 2, 2, Y, X), F32),
            vm((2, 2, 2, Y, X), F32),
            dma((Z + 9,)),
            dma((18,)),
            dma((18,)),
        ],
        compiler_params=pltpu.CompilerParams(
            collective_id=0, has_side_effects=True, vmem_limit_bytes=48 * 1024 * 1024
        ),
    )(*[pltpu.with_memory_space_constraint(v, pltpu.HBM) for v in (features, row(s1), row(t1), w1, row(b1), row(s2), row(t2), w2, row(b2), fw)])


def solution(mesh):
    return jax.shard_map(
        block,
        mesh=mesh,
        in_specs=(P(None, "gz", "gy", None), P(), P(), P(), P(), P(), P(), P(), P(), P()),
        out_specs=P(None, "gz", "gy", None),
        check_vma=False,
    )
```

```python
import jax
import jax.numpy as jnp
from jax import lax
from jax.experimental import pallas as pl
from jax.experimental.pallas import tpu as pltpu
from jax.sharding import PartitionSpec as P

MESH = pl.DeviceIdType.MESH
F32 = jnp.float32
BF16 = jnp.bfloat16
C = 32
Z = 4
Y = 8
X = 256
R = C * Y
G = 4


def iota(shape, dim):
    return lax.broadcasted_iota(jnp.int32, shape, dim)


def dot(a, b):
    return jnp.dot(a, b, preferred_element_type=F32)


def one_hot(flags):
    return jnp.where(flags, 1.0, 0.0).astype(BF16)


def from_left(value):
    moved = pltpu.roll(value, 1, axis=1)
    return jnp.where(iota(value.shape, 1) == 0, 0.0, moved)


def from_right(value):
    last = value.shape[1] - 1
    moved = pltpu.roll(value, last, axis=1)
    return jnp.where(iota(value.shape, 1) == last, 0.0, moved)


def kernel(
    x_hbm, s1_hbm, t1_hbm, w1_hbm, b1_hbm, s2_hbm, t2_hbm, w2_hbm, b2_hbm, fw_hbm,
    out,
    xin, par, w1, w2, fw, raw, ux, edge, ez, halo,
    cols, cols_e, wxy, wxz, wyz, wxy_e, wyz_e, whx, why, bxy, bxz, byz, bxy_e, byz_e, fres,
    hid, hid_e, acc, sm,
    rel, zs_, zr, rz, ys, yr,
    lsem, ssem, rsem,
):
    gz, gy = lax.axis_index("gz"), lax.axis_index("gy")
    nz, ny = lax.axis_size("gz"), lax.axis_size("gy")
    has_z = (gz > 0, gz < nz - 1)
    has_y = (gy > 0, gy < ny - 1)
    z_of = (gz - 1, gz + 1)
    y_of = (gy - 1, gy + 1)
    place = gy % G
    far = (has_y[0] & (place == 0), has_y[1] & (place == G - 1))
    way = (gy + G - 1, gy - G + 1)
    helps = ((place == G - 1) & (gy >= G), (place == 0) & (gy + G < ny))
    source = (gy - G + 1, gy + G - 1)
    beyond_group = (gy - G, gy + G)

    barrier = pltpu.get_barrier_semaphore()
    for side in range(2):
        @pl.when(has_z[side])
        def _():
            pl.semaphore_signal(barrier, inc=1, device_id=(z_of[side], gy), device_id_type=MESH)

        @pl.when(has_y[side])
        def _():
            pl.semaphore_signal(barrier, inc=1, device_id=(gz, y_of[side]), device_id_type=MESH)

        @pl.when(helps[side])
        def _():
            pl.semaphore_signal(barrier, inc=1, device_id=(gz, source[side]), device_id_type=MESH)

    order = (0, 3, 1, 2)
    loads = {z: pltpu.make_async_copy(x_hbm.at[:, z], xin.at[:, z], lsem.at[z]) for z in order}
    params = [
        pltpu.make_async_copy(source, par.at[i], lsem.at[Z + i])
        for i, source in enumerate((s1_hbm, t1_hbm, b1_hbm, s2_hbm, t2_hbm, b2_hbm))
    ]
    weights = [
        pltpu.make_async_copy(source, target, lsem.at[Z + 6 + i])
        for i, (source, target) in enumerate(((w1_hbm, w1), (w2_hbm, w2), (fw_hbm, fw)))
    ]
    for copy in (*params, loads[0], loads[3], loads[1], loads[2], *weights):
        copy.start()

    for side in range(2):
        slot = (0, Z + 1)[side]

        @pl.when(jnp.logical_not(has_z[side]))
        def _():
            ux[slot, 1] = jnp.zeros((R, X), BF16)
            halo[slot] = jnp.zeros((2, C, X), BF16)

        @pl.when(jnp.logical_not(has_y[side]))
        def _():
            for ze in range(1, Z + 1):
                halo[ze, side] = jnp.zeros((C, X), BF16)

        for yside in range(2):
            @pl.when(has_z[side] & jnp.logical_not(has_y[yside]))
            def _():
                halo[slot, yside] = jnp.zeros((C, X), BF16)

    for copy in params:
        copy.wait()
    pick = iota((R, C), 0) // Y == iota((R, C), 1)

    def column(row):
        return jnp.sum(jnp.where(pick, row, 0.0), axis=1, keepdims=True)

    b1_row, s2_row, t2_row, b2_row = par[2], par[3], par[4], par[5]
    cols[0] = jnp.broadcast_to(column(par[0]), (R, 128))
    cols[1] = jnp.broadcast_to(column(par[1]), (R, 128))
    cols[2] = jnp.broadcast_to(column(s2_row), (R, 128))
    cols[3] = jnp.broadcast_to(column(b1_row * s2_row + t2_row), (R, 128))

    pick_e = iota((2 * C, C), 0) % C == iota((2 * C, C), 1)
    cols_e[0] = jnp.broadcast_to(
        jnp.sum(jnp.where(pick_e, s2_row, 0.0), axis=1, keepdims=True), (2 * C, 128)
    )
    cols_e[1] = jnp.broadcast_to(
        jnp.sum(jnp.where(pick_e, b1_row * s2_row + t2_row, 0.0), axis=1, keepdims=True), (2 * C, 128)
    )

    def wide(half):
        return jnp.concatenate([half, half], axis=1)

    rows, lanes = iota((2 * C, R), 0), iota((2 * C, R), 1)
    edge_pick = one_hot(lanes == (rows % C) * Y + (rows // C) * (Y - 1))
    for z in order:
        loads[z].wait()
        value = xin[:, z].astype(F32).reshape(R, X)
        raw[z] = value.astype(BF16)
        unit = jnp.maximum(value * wide(cols[0]) + wide(cols[1]), 0.0).astype(BF16)
        ux[z + 1, 1] = unit
        edge[z] = dot(edge_pick, unit).astype(BF16).reshape(2, C, X)

    def remote(source, target, i, zi, yi):
        return pltpu.make_async_remote_copy(
            src_ref=source, dst_ref=target, send_sem=ssem.at[i], recv_sem=rsem.at[i],
            device_id=(zi, yi), device_id_type=MESH,
        )

    send_ez = [remote(edge.at[(0, Z - 1)[s]], ez.at[1 - s], s, z_of[s], gy) for s in range(2)]
    send_slab = [
        remote(ux.at[(1, Z)[s], 1], ux.at[(Z + 1, 0)[s], 1], 2 + s, z_of[s], gy) for s in range(2)
    ]
    send_y = [
        [remote(edge.at[z, s], halo.at[z + 1, 1 - s], 4 + s * Z + z, gz, y_of[s]) for z in range(Z)]
        for s in range(2)
    ]
    send_way = [
        [remote(edge.at[z, s], rel.at[s, z], 16 + s * (Z - 1) + z, gz, way[s]) for z in range(Z - 1)]
        for s in range(2)
    ]
    pass_on = [
        [
            pltpu.make_async_remote_copy(
                src_ref=rel.at[s, z], dst_ref=halo.at[z + 1, 1 - s], send_sem=ssem.at[28 + s * (Z - 1) + z],
                recv_sem=rsem.at[4 + s * Z + z], device_id=(gz, beyond_group[s]), device_id_type=MESH,
            )
            for z in range(Z - 1)
        ]
        for s in range(2)
    ]
    send_corner = [
        [
            remote(ez.at[zs, ys_], halo.at[(0, Z + 1)[zs], 1 - ys_], 12 + 2 * zs + ys_, gz, y_of[ys_])
            for ys_ in range(2)
        ]
        for zs in range(2)
    ]

    def relay(s):
        @pl.when(helps[s])
        def _():
            for z in range(Z - 1):
                send_way[s][z].wait_recv()
                pass_on[s][z].start()

    for copy in weights:
        copy.wait()
    spread = one_hot(iota((C, R), 1) // Y == iota((C, R), 0))
    repeat = one_hot(pick)
    wide_w1 = dot(w1[...].reshape(9 * C, C), spread).astype(BF16)
    shift = iota((R, R), 1) % Y - iota((R, R), 0) % Y
    for j in range(3):
        banded = None
        for i in range(3):
            k = 3 * i + j
            full = dot(repeat, wide_w1[k * C : (k + 1) * C])
            term = jnp.where(shift == i - 1, full, 0.0)
            banded = term if banded is None else banded + term
            wxz[i, :, j * R : (j + 1) * R] = jnp.where(shift == 0, full, 0.0).astype(BF16)
        wxy[:, j * R : (j + 1) * R] = banded.astype(BF16)
    for i in range(3):
        banded = None
        for j in range(3):
            k = 3 * i + j
            full = dot(repeat, wide_w1[k * C : (k + 1) * C])
            term = jnp.where(shift == j - 1, full, 0.0)
            banded = term if banded is None else banded + term
        wyz[i] = banded.astype(BF16)
    for i in range(3):
        wyz_e[i] = dot(edge_pick, wyz[i]).astype(BF16)
    wxy_e[...] = dot(edge_pick, wxy[...]).astype(BF16)
    reach = 6 * C
    touched = iota((2 * C, reach), 0) // C == (iota((2 * C, reach), 1) // C) % 2
    repeat_e = one_hot(pick_e)
    packed_x = jnp.zeros((C, reach), F32)
    packed_y = jnp.zeros((C, reach), F32)
    for tap in range(3):
        for side in range(2):
            put = one_hot(iota((C, reach), 1) == iota((C, reach), 0) + (2 * tap + side) * C)
            packed_x += dot(w1[2 * side, tap], put)
            packed_y += dot(w1[tap, 2 * side], put)
    whx[...] = jnp.where(touched, dot(repeat_e, packed_x.astype(BF16)), 0.0).astype(BF16)
    why[...] = jnp.where(touched, dot(repeat_e, packed_y.astype(BF16)), 0.0).astype(BF16)

    rows, lanes = iota((2 * 16, R), 0) % 16, iota((2 * 16, R), 1) % Y
    first = jnp.broadcast_to(fw[0:1, :].astype(F32), (16, C))
    second = jnp.broadcast_to(fw[1:2, :].astype(F32), (16, C))
    fw32 = jnp.concatenate([first, second], axis=0)
    fw16 = jnp.concatenate([first[:Y], second[:Y]], axis=0)
    highs, lows = [], []
    for i in range(3):
        for j in range(3):
            g = dot(fw32.astype(BF16), w2[i, j])
            high = g.astype(BF16)
            highs.append(high)
            lows.append((g - high.astype(F32)).astype(BF16))
    taps = dot(jnp.concatenate(highs + lows, axis=0), spread).reshape(2, 3, 3, 32, R)
    same = rows == lanes
    for part in range(2):
        for a in range(3):
            band_xy = jnp.zeros((32, R), F32)
            band_yz = jnp.zeros((32, R), F32)
            for b in range(3):
                hit = rows == (lanes + (17 - b)) % 16
                band_xy += jnp.where(hit, taps[part, b, a], 0.0)
                band_yz += jnp.where(hit, taps[part, a, b], 0.0)
            at = (part * 3 + a) * 32
            bxy[at : at + 32, :] = band_xy.astype(BF16)
            byz[at : at + 32, :] = band_yz.astype(BF16)
        for i in range(3):
            for j in range(3):
                value = jnp.where(same, taps[part, i, j], 0.0)
                at = (part * 9 + i * 3 + j) * 16
                bxz[at : at + 16, :] = jnp.concatenate([value[:Y], value[16 : 16 + Y]], axis=0).astype(BF16)
    rows, lanes = iota((R, 2 * C), 0), iota((R, 2 * C), 1)
    edge_put = one_hot(rows == (lanes % C) * Y + (lanes // C) * (Y - 1))
    bxy_e[...] = dot(bxy[...], edge_put).astype(BF16)
    byz_e[...] = dot(byz[...], edge_put).astype(BF16)
    own = iota((16, R), 0) % Y == iota((16, R), 1) % Y
    fres[...] = jnp.where(own, dot(fw16.astype(BF16), spread), 0.0).astype(BF16)
    bias = jnp.sum(fw16 * b2_row, axis=1, keepdims=True)

    peers = sum(flag.astype(jnp.int32) for flag in (*has_z, *has_y, *far))
    pl.semaphore_wait(barrier, peers)

    for side in range(2):
        @pl.when(has_z[side])
        def _():
            send_ez[side].start()
    for side in range(2):
        @pl.when(far[side])
        def _():
            for z in range(Z - 1):
                send_way[side][z].start()
            send_y[side][Z - 1].start()

        @pl.when(has_y[side] & jnp.logical_not(far[side]))
        def _():
            for z in range(Z):
                send_y[side][z].start()
    for side in range(2):
        @pl.when(has_z[side])
        def _():
            send_slab[side].start()

    def shifted(ze):
        value = ux[ze, 1].astype(F32)
        ux[ze, 0] = from_left(value).astype(BF16)
        ux[ze, 2] = from_right(value).astype(BF16)

    for ze in range(1, Z + 1):
        shifted(ze)

    row8 = iota((R, X), 0) % Y
    inner = (row8 > 0) & (row8 < Y - 1)

    def active(hidden):
        return jnp.maximum(hidden * wide(cols[2]) + wide(cols[3]), 0.0)

    def active_e(hidden):
        return jnp.maximum(hidden * wide(cols_e[0]) + wide(cols_e[1]), 0.0).astype(BF16)

    def add_xy(z, both):
        part = (both[:96] + both[96:]).reshape(3, 2, 2, Y, X)
        for j in range(3):
            acc[j, z + 1, 1] += part[j, 0]
            acc[j, z + 1, 2] += part[j, 1]

    def add_yz(z, both):
        part = (both[:96] + both[96:]).reshape(3, 2, 2, Y, X)
        for i in range(3):
            acc[1, z + 2 - i, 0] += part[i, 0]
            acc[1, z + 2 - i, 1] += part[i, 1]

    acc[...] = jnp.zeros_like(acc)
    for z in range(Z):
        wide_x = ux[z + 1].reshape(3 * R, X)
        hid_e[0, z] = dot(wxy_e[...], wide_x)
        value = jnp.where(inner, active(dot(wxy[...], wide_x)), 0.0).astype(BF16)
        add_xy(z, dot(bxy[...], value))

    for side in range(2):
        @pl.when(has_z[side])
        def _():
            send_ez[side].wait_send()
            send_ez[1 - side].wait_recv()
            for yside in range(2):
                @pl.when(has_y[yside])
                def _():
                    send_corner[side][yside].start()

    relay(0)

    for z in range(Z):
        xz = dot(wxz[1], ux[z + 1].reshape(3 * R, X))
        yz = dot(wyz[1], ux[z + 1, 1])
        yz_e = dot(wyz_e[1], ux[z + 1, 1])
        for i in (0, 2):
            if 1 <= z + i <= Z:
                xz += dot(wxz[i], ux[z + i].reshape(3 * R, X))
                yz += dot(wyz[i], ux[z + i, 1])
                yz_e += dot(wyz_e[i], ux[z + i, 1])
        hid[0, z] = xz
        hid[1, z] = yz
        hid_e[1, z] = yz_e
        residual = dot(fres[...], raw[z]) + bias
        r0, r1 = residual[:Y], residual[Y:]
        acc[1, z + 1, 0, 0] += 2.0 * r0
        acc[1, z + 1, 1, 0] += r0 + r1
        acc[1, z + 1, 2, 0] += 2.0 * r1

    def finish(z):
        both = dot(bxz[...], active(hid[0, z]).astype(BF16))
        part = both[:144] + both[144:]
        for i in range(3):
            for j in range(3):
                at = (i * 3 + j) * 16
                acc[j, z + 2 - i, 0, 0] += part[at : at + Y]
                acc[j, z + 2 - i, 2, 0] += part[at + Y : at + 16]
        add_yz(z, dot(byz[...], jnp.where(inner, active(hid[1, z]), 0.0).astype(BF16)))

    for z in range(1, Z - 1):
        finish(z)

    relay(1)

    for side in range(2):
        @pl.when(has_z[side])
        def _():
            send_slab[1 - side].wait_recv()
    for ze in (0, Z + 1):
        shifted(ze)
    for z, i in ((0, 0), (Z - 1, 2)):
        hid[0, z] += dot(wxz[i], ux[z + i].reshape(3 * R, X))
        hid[1, z] += dot(wyz[i], ux[z + i, 1])
        hid_e[1, z] += dot(wyz_e[i], ux[z + i, 1])
        finish(z)

    for side in range(2):
        @pl.when(has_y[side])
        def _():
            for z in range(Z):
                send_y[1 - side][z].wait_recv()
    hidden = []
    for z in range(Z):
        beside = halo[z + 1].reshape(2 * C, X)
        wider = beside.astype(F32)
        three = jnp.concatenate([from_left(wider).astype(BF16), beside, from_right(wider).astype(BF16)], axis=0)
        hidden.append(hid_e[0, z] + dot(whx[...], three))
    both = [dot(bxy_e[...], active_e(value)) for value in hidden]
    for z in range(Z):
        add_xy(z, both[z])
    for side in range(2):
        @pl.when(has_y[side])
        def _():
            for zside in range(2):
                @pl.when(has_z[zside])
                def _():
                    send_corner[zside][1 - side].wait_recv()
    hidden = [hid_e[1, z] + dot(why[...], halo[z : z + 3].reshape(6 * C, X)) for z in range(Z)]
    both = [dot(byz_e[...], active_e(value)) for value in hidden]
    for z in range(Z):
        add_yz(z, both[z])

    rows16x = iota((16, X), 0)
    outside = ((rows16x == 15) & jnp.logical_not(has_y[0])) | ((rows16x == Y) & jnp.logical_not(has_y[1]))
    flow = {}
    for ze in range(Z + 2):
        for comp in range(3):
            value = (
                from_left(acc[0, ze, comp].reshape(16, X))
                + acc[1, ze, comp].reshape(16, X)
                + from_right(acc[2, ze, comp].reshape(16, X))
            )
            value = jnp.where(outside, 0.0, value)
            if ze == 0:
                value = jnp.where(has_z[0], value, 0.0)
            if ze == Z + 1:
                value = jnp.where(has_z[1], value, 0.0)
            value = 0.125 * (from_left(value) + from_right(value)) + 0.25 * value
            flow[ze, comp] = 0.5 * value + 0.25 * (pltpu.roll(value, 1, axis=0) + pltpu.roll(value, 15, axis=0))
    for comp in range(3):
        for zs in range(Z + 4):
            value = None
            for ze, weight in ((zs - 2, 0.25), (zs - 1, 0.5), (zs, 0.25)):
                if 0 <= ze < Z + 2:
                    term = weight * flow[ze, comp]
                    value = term if value is None else value + term
            sm[0, zs, comp] = value[:Y]
            sm[1, zs, comp] = value[Y:]

    send_zr = [remote(zs_.at[t], zr.at[1 - t], 22 + t, z_of[t], gy) for t in range(2)]
    send_rz = [remote(sm.at[0, pl.ds((0, Z + 2)[t], 2)], rz.at[1 - t], 24 + t, z_of[t], gy) for t in range(2)]
    send_ry = [remote(ys.at[s], yr.at[1 - s], 26 + s, gz, y_of[s]) for s in range(2)]
    row = iota((Y, X), 0)
    low, high = row < 2, row >= Y - 2

    def moved(value, by):
        return pltpu.roll(value, by % Y, axis=0) if by % Y else value

    for t in range(2):
        for comp in range(3):
            a, b = sm[1, (0, Z + 2)[t], comp], sm[1, (0, Z + 2)[t] + 1, comp]
            kept = jnp.where(low, a, jnp.where(high, b, 0.0))
            zs_[t, comp] = kept + moved(jnp.where(high, a, jnp.where(low, b, 0.0)), 4)

        @pl.when(has_z[t])
        def _():
            send_zr[t].start()

    for side in range(2):
        @pl.when(jnp.logical_not(has_z[side]))
        def _():
            zr[side] = jnp.zeros((3, Y, X), F32)
            rz[side] = jnp.zeros((2, 3, Y, X), F32)

        @pl.when(jnp.logical_not(has_y[side]))
        def _():
            yr[side] = jnp.zeros((4 * Y, X), BF16)

    for side in range(2):
        @pl.when(has_z[side])
        def _():
            send_zr[1 - side].wait_recv()
    packs = [[], []]
    for comp in range(3):
        up, down = None, None
        for z in range(Z):
            value = zr[z // 2, comp]
            turned = moved(value, 4)
            if z % 2 == 0:
                value = jnp.where(low, value, turned)
            else:
                value = jnp.where(low, turned, value)
            value = sm[1, z + 2, comp] + value
            first = moved(jnp.where(low, value, 0.0), 2 * z)
            last = moved(jnp.where(high, value, 0.0), 2 * z + 2)
            up = first if up is None else up + first
            down = last if down is None else down + last
        packs[1].append(up)
        packs[0].append(down)
    for s in range(2):
        ys[s] = jnp.concatenate([*packs[s], jnp.zeros((Y, X), F32)], axis=0).astype(BF16)

        @pl.when(has_y[s])
        def _():
            send_ry[s].start()
    for t in range(2):
        @pl.when(has_z[t])
        def _():
            send_rz[t].start()

    for side in range(2):
        @pl.when(has_z[side])
        def _():
            send_rz[1 - side].wait_recv()
    for comp in range(3):
        for z in range(Z):
            sm[0, z + 2, comp] += rz[z // 2, z % 2, comp]
    for side in range(2):
        @pl.when(has_y[side])
        def _():
            send_ry[1 - side].wait_recv()
    came = [yr[s].astype(F32) for s in range(2)]
    for comp in range(3):
        for z in range(Z):
            first = moved(came[0][comp * Y : (comp + 1) * Y], -2 * z)
            last = moved(came[1][comp * Y : (comp + 1) * Y], -2 - 2 * z)
            value = jnp.where(low, first, jnp.where(high, last, 0.0))
            out[comp, z] = sm[0, z + 2, comp] + value

    for side in range(2):
        @pl.when(has_z[side])
        def _():
            send_slab[side].wait_send()
            send_zr[side].wait_send()
            send_rz[side].wait_send()

        @pl.when(far[side])
        def _():
            for z in range(Z - 1):
                send_way[side][z].wait_send()
            send_y[side][Z - 1].wait_send()

        @pl.when(has_y[side] & jnp.logical_not(far[side]))
        def _():
            for z in range(Z):
                send_y[side][z].wait_send()

        @pl.when(helps[side])
        def _():
            for z in range(Z - 1):
                pass_on[side][z].wait_send()

        @pl.when(has_y[side])
        def _():
            send_ry[side].wait_send()

        for s in range(2):
            @pl.when(has_z[side] & has_y[s])
            def _():
                send_corner[side][s].wait_send()


def block(features, s1, t1, w1, b1, s2, t2, w2, b2, fw):
    def row(v):
        return v.reshape(1, C)

    vm = pltpu.VMEM
    dma = pltpu.SemaphoreType.DMA
    return pl.pallas_call(
        kernel,
        out_shape=pltpu.VMEM((3, Z, Y, X), F32),
        in_specs=[pl.BlockSpec(memory_space=pltpu.HBM)] * 10,
        out_specs=pl.BlockSpec(memory_space=pltpu.VMEM),
        scratch_shapes=[
            vm((C, Z, Y, X), BF16),
            vm((6, 1, C), F32),
            vm((3, 3, C, C), BF16),
            vm((3, 3, C, C), BF16),
            vm((2, C), BF16),
            vm((Z, R, X), BF16),
            vm((Z + 2, 3, R, X), BF16),
            vm((Z, 2, C, X), BF16),
            vm((2, 2, C, X), BF16),
            vm((Z + 2, 2, C, X), BF16),
            vm((4, R, 128), F32),
            vm((2, 2 * C, 128), F32),
            vm((R, 3 * R), BF16),
            vm((3, R, 3 * R), BF16),
            vm((3, R, R), BF16),
            vm((2 * C, 3 * R), BF16),
            vm((3, 2 * C, R), BF16),
            vm((2 * C, 6 * C), BF16),
            vm((2 * C, 6 * C), BF16),
            vm((192, R), BF16),
            vm((288, R), BF16),
            vm((192, R), BF16),
            vm((192, 2 * C), BF16),
            vm((192, 2 * C), BF16),
            vm((16, R), BF16),
            vm((2, Z, R, X), F32),
            vm((2, Z, 2 * C, X), F32),
            vm((3, Z + 2, 3, 2, Y, X), F32),
            vm((2, Z + 4, 3, Y, X), F32),
            vm((2, Z - 1, C, X), BF16),
            vm((2, 3, Y, X), F32),
            vm((2, 3, Y, X), F32),
            vm((2, 2, 3, Y, X), F32),
            vm((2, 4 * Y, X), BF16),
            vm((2, 4 * Y, X), BF16),
            dma((Z + 9,)),
            dma((34,)),
            dma((34,)),
        ],
        compiler_params=pltpu.CompilerParams(
            collective_id=0, has_side_effects=True, vmem_limit_bytes=48 * 1024 * 1024
        ),
    )(*[pltpu.with_memory_space_constraint(v, pltpu.HBM) for v in (features, row(s1), row(t1), w1, row(b1), row(s2), row(t2), w2, row(b2), fw)])


def solution(mesh):
    return jax.shard_map(
        block,
        mesh=mesh,
        in_specs=(P(None, "gz", "gy", None), P(), P(), P(), P(), P(), P(), P(), P(), P()),
        out_specs=P(None, "gz", "gy", None),
        check_vma=False,
    )
```

```python
import jax
import jax.numpy as jnp
from jax import lax
from jax.experimental import pallas as pl
from jax.experimental.pallas import tpu as pltpu
from jax.sharding import PartitionSpec as P

MESH = pl.DeviceIdType.MESH
F32 = jnp.float32
BF16 = jnp.bfloat16
C = 32
Z = 4
Y = 8
X = 256
R = C * Y
K = 2
G = 4


def iota(shape, dim):
    return lax.broadcasted_iota(jnp.int32, shape, dim)


def dot(a, b):
    return jnp.dot(a, b, preferred_element_type=F32)


def one_hot(flags):
    return jnp.where(flags, 1.0, 0.0).astype(BF16)


def from_left(value):
    moved = pltpu.roll(value, 1, axis=1)
    return jnp.where(iota(value.shape, 1) == 0, 0.0, moved)


def from_right(value):
    last = value.shape[1] - 1
    moved = pltpu.roll(value, last, axis=1)
    return jnp.where(iota(value.shape, 1) == last, 0.0, moved)


def kernel(
    x_hbm, s1_hbm, t1_hbm, w1_hbm, b1_hbm, s2_hbm, t2_hbm, w2_hbm, b2_hbm, fw_hbm,
    out,
    xin, par, w1, w2, fw, raw, ux, edge, ez, halo,
    cols, cols_e, wxy, wxz, wyz, wxy_e, wyz_e, whx, why, bxy, bxz, byz, bxy_e, byz_e, fres,
    hid, hid_e, acc, sm,
    rel, zs_, zr, rz, ys, yr,
    lsem, ssem, rsem,
):
    gz, gy = lax.axis_index("gz"), lax.axis_index("gy")
    nz, ny = lax.axis_size("gz"), lax.axis_size("gy")
    has_z = (gz > 0, gz < nz - 1)
    has_y = (gy > 0, gy < ny - 1)
    z_of = (gz - 1, gz + 1)
    y_of = (gy - 1, gy + 1)
    place = gy % G
    far = (has_y[0] & (place == 0), has_y[1] & (place == G - 1))
    way = (gy + G - 1, gy - G + 1)
    helps = ((place == G - 1) & (gy >= G), (place == 0) & (gy + G < ny))
    source = (gy - G + 1, gy + G - 1)
    beyond_group = (gy - G, gy + G)

    barrier = pltpu.get_barrier_semaphore()
    for side in range(2):
        @pl.when(has_z[side])
        def _():
            pl.semaphore_signal(barrier, inc=1, device_id=(z_of[side], gy), device_id_type=MESH)

        @pl.when(has_y[side])
        def _():
            pl.semaphore_signal(barrier, inc=1, device_id=(gz, y_of[side]), device_id_type=MESH)

        @pl.when(helps[side])
        def _():
            pl.semaphore_signal(barrier, inc=1, device_id=(gz, source[side]), device_id_type=MESH)

    order = (0, 3, 1, 2)
    loads = {z: pltpu.make_async_copy(x_hbm.at[:, z], xin.at[:, z], lsem.at[z]) for z in order}
    params = [
        pltpu.make_async_copy(source, par.at[i], lsem.at[Z + i])
        for i, source in enumerate((s1_hbm, t1_hbm, b1_hbm, s2_hbm, t2_hbm, b2_hbm))
    ]
    weights = [
        pltpu.make_async_copy(source, target, lsem.at[Z + 6 + i])
        for i, (source, target) in enumerate(((w1_hbm, w1), (w2_hbm, w2), (fw_hbm, fw)))
    ]
    for copy in (*params, loads[0], loads[3], loads[1], loads[2], *weights):
        copy.start()

    for side in range(2):
        slot = (0, Z + 1)[side]

        @pl.when(jnp.logical_not(has_z[side]))
        def _():
            ux[slot, 1] = jnp.zeros((R, X), BF16)
            halo[slot] = jnp.zeros((2, C, X), BF16)

        @pl.when(jnp.logical_not(has_y[side]))
        def _():
            for ze in range(1, Z + 1):
                halo[ze, side] = jnp.zeros((C, X), BF16)

        for yside in range(2):
            @pl.when(has_z[side] & jnp.logical_not(has_y[yside]))
            def _():
                halo[slot, yside] = jnp.zeros((C, X), BF16)

    for copy in params:
        copy.wait()
    pick = iota((R, C), 0) // Y == iota((R, C), 1)

    def column(row):
        return jnp.sum(jnp.where(pick, row, 0.0), axis=1, keepdims=True)

    b1_row, s2_row, t2_row, b2_row = par[2], par[3], par[4], par[5]
    cols[0] = jnp.broadcast_to(column(par[0]), (R, 128))
    cols[1] = jnp.broadcast_to(column(par[1]), (R, 128))
    cols[2] = jnp.broadcast_to(column(s2_row), (R, 128))
    cols[3] = jnp.broadcast_to(column(b1_row * s2_row + t2_row), (R, 128))

    pick_e = iota((2 * C, C), 0) % C == iota((2 * C, C), 1)
    cols_e[0] = jnp.broadcast_to(
        jnp.sum(jnp.where(pick_e, s2_row, 0.0), axis=1, keepdims=True), (2 * C, 128)
    )
    cols_e[1] = jnp.broadcast_to(
        jnp.sum(jnp.where(pick_e, b1_row * s2_row + t2_row, 0.0), axis=1, keepdims=True), (2 * C, 128)
    )

    def wide(half):
        return jnp.concatenate([half, half], axis=1)

    rows, lanes = iota((2 * C, R), 0), iota((2 * C, R), 1)
    edge_pick = one_hot(lanes == (rows % C) * Y + (rows // C) * (Y - 1))
    for z in order:
        loads[z].wait()
        value = xin[:, z].astype(F32).reshape(R, X)
        raw[z] = value.astype(BF16)
        unit = jnp.maximum(value * wide(cols[0]) + wide(cols[1]), 0.0).astype(BF16)
        ux[z + 1, 1] = unit
        edge[z] = dot(edge_pick, unit).astype(BF16).reshape(2, C, X)

    def remote(source, target, i, zi, yi):
        return pltpu.make_async_remote_copy(
            src_ref=source, dst_ref=target, send_sem=ssem.at[i], recv_sem=rsem.at[i],
            device_id=(zi, yi), device_id_type=MESH,
        )

    send_ez = [remote(edge.at[(0, Z - 1)[s]], ez.at[1 - s], s, z_of[s], gy) for s in range(2)]
    send_slab = [
        remote(ux.at[(1, Z)[s], 1], ux.at[(Z + 1, 0)[s], 1], 2 + s, z_of[s], gy) for s in range(2)
    ]
    send_y = [
        [remote(edge.at[z, s], halo.at[z + 1, 1 - s], 4 + s * Z + z, gz, y_of[s]) for z in range(Z)]
        for s in range(2)
    ]
    send_way = [
        [remote(edge.at[z, s], rel.at[s, z], 16 + s * (Z - 1) + z, gz, way[s]) for z in range(K)]
        for s in range(2)
    ]
    pass_on = [
        [
            pltpu.make_async_remote_copy(
                src_ref=rel.at[s, z], dst_ref=halo.at[z + 1, 1 - s], send_sem=ssem.at[28 + s * (Z - 1) + z],
                recv_sem=rsem.at[4 + s * Z + z], device_id=(gz, beyond_group[s]), device_id_type=MESH,
            )
            for z in range(K)
        ]
        for s in range(2)
    ]
    send_corner = [
        [
            remote(ez.at[zs, ys_], halo.at[(0, Z + 1)[zs], 1 - ys_], 12 + 2 * zs + ys_, gz, y_of[ys_])
            for ys_ in range(2)
        ]
        for zs in range(2)
    ]

    def relay(s):
        @pl.when(helps[s])
        def _():
            for z in range(K):
                send_way[s][z].wait_recv()
                pass_on[s][z].start()

    for copy in weights:
        copy.wait()
    spread = one_hot(iota((C, R), 1) // Y == iota((C, R), 0))
    repeat = one_hot(pick)
    wide_w1 = dot(w1[...].reshape(9 * C, C), spread).astype(BF16)
    shift = iota((R, R), 1) % Y - iota((R, R), 0) % Y
    for j in range(3):
        banded = None
        for i in range(3):
            k = 3 * i + j
            full = dot(repeat, wide_w1[k * C : (k + 1) * C])
            term = jnp.where(shift == i - 1, full, 0.0)
            banded = term if banded is None else banded + term
            wxz[i, :, j * R : (j + 1) * R] = jnp.where(shift == 0, full, 0.0).astype(BF16)
        wxy[:, j * R : (j + 1) * R] = banded.astype(BF16)
    for i in range(3):
        banded = None
        for j in range(3):
            k = 3 * i + j
            full = dot(repeat, wide_w1[k * C : (k + 1) * C])
            term = jnp.where(shift == j - 1, full, 0.0)
            banded = term if banded is None else banded + term
        wyz[i] = banded.astype(BF16)
    for i in range(3):
        wyz_e[i] = dot(edge_pick, wyz[i]).astype(BF16)
    wxy_e[...] = dot(edge_pick, wxy[...]).astype(BF16)
    reach = 6 * C
    touched = iota((2 * C, reach), 0) // C == (iota((2 * C, reach), 1) // C) % 2
    repeat_e = one_hot(pick_e)
    packed_x = jnp.zeros((C, reach), F32)
    packed_y = jnp.zeros((C, reach), F32)
    for tap in range(3):
        for side in range(2):
            put = one_hot(iota((C, reach), 1) == iota((C, reach), 0) + (2 * tap + side) * C)
            packed_x += dot(w1[2 * side, tap], put)
            packed_y += dot(w1[tap, 2 * side], put)
    whx[...] = jnp.where(touched, dot(repeat_e, packed_x.astype(BF16)), 0.0).astype(BF16)
    why[...] = jnp.where(touched, dot(repeat_e, packed_y.astype(BF16)), 0.0).astype(BF16)

    rows, lanes = iota((2 * 16, R), 0) % 16, iota((2 * 16, R), 1) % Y
    first = jnp.broadcast_to(fw[0:1, :].astype(F32), (16, C))
    second = jnp.broadcast_to(fw[1:2, :].astype(F32), (16, C))
    fw32 = jnp.concatenate([first, second], axis=0)
    fw16 = jnp.concatenate([first[:Y], second[:Y]], axis=0)
    highs, lows = [], []
    for i in range(3):
        for j in range(3):
            g = dot(fw32.astype(BF16), w2[i, j])
            high = g.astype(BF16)
            highs.append(high)
            lows.append((g - high.astype(F32)).astype(BF16))
    taps = dot(jnp.concatenate(highs + lows, axis=0), spread).reshape(2, 3, 3, 32, R)
    same = rows == lanes
    for part in range(2):
        for a in range(3):
            band_xy = jnp.zeros((32, R), F32)
            band_yz = jnp.zeros((32, R), F32)
            for b in range(3):
                hit = rows == (lanes + (17 - b)) % 16
                band_xy += jnp.where(hit, taps[part, b, a], 0.0)
                band_yz += jnp.where(hit, taps[part, a, b], 0.0)
            at = (part * 3 + a) * 32
            bxy[at : at + 32, :] = band_xy.astype(BF16)
            byz[at : at + 32, :] = band_yz.astype(BF16)
        for i in range(3):
            for j in range(3):
                value = jnp.where(same, taps[part, i, j], 0.0)
                at = (part * 9 + i * 3 + j) * 16
                bxz[at : at + 16, :] = jnp.concatenate([value[:Y], value[16 : 16 + Y]], axis=0).astype(BF16)
    rows, lanes = iota((R, 2 * C), 0), iota((R, 2 * C), 1)
    edge_put = one_hot(rows == (lanes % C) * Y + (lanes // C) * (Y - 1))
    bxy_e[...] = dot(bxy[...], edge_put).astype(BF16)
    byz_e[...] = dot(byz[...], edge_put).astype(BF16)
    own = iota((16, R), 0) % Y == iota((16, R), 1) % Y
    fres[...] = jnp.where(own, dot(fw16.astype(BF16), spread), 0.0).astype(BF16)
    bias = jnp.sum(fw16 * b2_row, axis=1, keepdims=True)

    peers = sum(flag.astype(jnp.int32) for flag in (*has_z, *has_y, *far))
    pl.semaphore_wait(barrier, peers)

    for side in range(2):
        @pl.when(has_z[side])
        def _():
            send_ez[side].start()
    for side in range(2):
        @pl.when(far[side])
        def _():
            for z in range(K):
                send_way[side][z].start()
            for z in range(K, Z):
                send_y[side][z].start()

        @pl.when(has_y[side] & jnp.logical_not(far[side]))
        def _():
            for z in range(Z):
                send_y[side][z].start()
    for side in range(2):
        @pl.when(has_z[side])
        def _():
            send_slab[side].start()

    def shifted(ze):
        value = ux[ze, 1].astype(F32)
        ux[ze, 0] = from_left(value).astype(BF16)
        ux[ze, 2] = from_right(value).astype(BF16)

    for ze in range(1, Z + 1):
        shifted(ze)

    row8 = iota((R, X), 0) % Y
    inner = (row8 > 0) & (row8 < Y - 1)

    def active(hidden):
        return jnp.maximum(hidden * wide(cols[2]) + wide(cols[3]), 0.0)

    def active_e(hidden):
        return jnp.maximum(hidden * wide(cols_e[0]) + wide(cols_e[1]), 0.0).astype(BF16)

    def add_xy(z, both):
        part = (both[:96] + both[96:]).reshape(3, 2, 2, Y, X)
        for j in range(3):
            acc[j, z + 1, 1] += part[j, 0]
            acc[j, z + 1, 2] += part[j, 1]

    def add_yz(z, both):
        part = (both[:96] + both[96:]).reshape(3, 2, 2, Y, X)
        for i in range(3):
            acc[1, z + 2 - i, 0] += part[i, 0]
            acc[1, z + 2 - i, 1] += part[i, 1]

    acc[...] = jnp.zeros_like(acc)
    relay(0)
    for z in range(Z):
        wide_x = ux[z + 1].reshape(3 * R, X)
        hid_e[0, z] = dot(wxy_e[...], wide_x)
        value = jnp.where(inner, active(dot(wxy[...], wide_x)), 0.0).astype(BF16)
        add_xy(z, dot(bxy[...], value))

    for side in range(2):
        @pl.when(has_z[side])
        def _():
            send_ez[side].wait_send()
            send_ez[1 - side].wait_recv()
            for yside in range(2):
                @pl.when(has_y[yside])
                def _():
                    send_corner[side][yside].start()

    for z in range(Z):
        xz = dot(wxz[1], ux[z + 1].reshape(3 * R, X))
        yz = dot(wyz[1], ux[z + 1, 1])
        yz_e = dot(wyz_e[1], ux[z + 1, 1])
        for i in (0, 2):
            if 1 <= z + i <= Z:
                xz += dot(wxz[i], ux[z + i].reshape(3 * R, X))
                yz += dot(wyz[i], ux[z + i, 1])
                yz_e += dot(wyz_e[i], ux[z + i, 1])
        hid[0, z] = xz
        hid[1, z] = yz
        hid_e[1, z] = yz_e
        residual = dot(fres[...], raw[z]) + bias
        r0, r1 = residual[:Y], residual[Y:]
        acc[1, z + 1, 0, 0] += 2.0 * r0
        acc[1, z + 1, 1, 0] += r0 + r1
        acc[1, z + 1, 2, 0] += 2.0 * r1

    def finish(z):
        both = dot(bxz[...], active(hid[0, z]).astype(BF16))
        part = both[:144] + both[144:]
        for i in range(3):
            for j in range(3):
                at = (i * 3 + j) * 16
                acc[j, z + 2 - i, 0, 0] += part[at : at + Y]
                acc[j, z + 2 - i, 2, 0] += part[at + Y : at + 16]
        add_yz(z, dot(byz[...], jnp.where(inner, active(hid[1, z]), 0.0).astype(BF16)))

    for z in range(1, Z - 1):
        finish(z)

    relay(1)

    for side in range(2):
        @pl.when(has_z[side])
        def _():
            send_slab[1 - side].wait_recv()
    for ze in (0, Z + 1):
        shifted(ze)
    for z, i in ((0, 0), (Z - 1, 2)):
        hid[0, z] += dot(wxz[i], ux[z + i].reshape(3 * R, X))
        hid[1, z] += dot(wyz[i], ux[z + i, 1])
        hid_e[1, z] += dot(wyz_e[i], ux[z + i, 1])
        finish(z)

    for side in range(2):
        @pl.when(has_y[side])
        def _():
            for z in range(Z):
                send_y[1 - side][z].wait_recv()
    hidden = []
    for z in range(Z):
        beside = halo[z + 1].reshape(2 * C, X)
        wider = beside.astype(F32)
        three = jnp.concatenate([from_left(wider).astype(BF16), beside, from_right(wider).astype(BF16)], axis=0)
        hidden.append(hid_e[0, z] + dot(whx[...], three))
    both = [dot(bxy_e[...], active_e(value)) for value in hidden]
    for z in range(Z):
        add_xy(z, both[z])
    for side in range(2):
        @pl.when(has_y[side])
        def _():
            for zside in range(2):
                @pl.when(has_z[zside])
                def _():
                    send_corner[zside][1 - side].wait_recv()
    hidden = [hid_e[1, z] + dot(why[...], halo[z : z + 3].reshape(6 * C, X)) for z in range(Z)]
    both = [dot(byz_e[...], active_e(value)) for value in hidden]
    for z in range(Z):
        add_yz(z, both[z])

    rows16x = iota((16, X), 0)
    outside = ((rows16x == 15) & jnp.logical_not(has_y[0])) | ((rows16x == Y) & jnp.logical_not(has_y[1]))
    flow = {}
    for ze in range(Z + 2):
        for comp in range(3):
            value = (
                from_left(acc[0, ze, comp].reshape(16, X))
                + acc[1, ze, comp].reshape(16, X)
                + from_right(acc[2, ze, comp].reshape(16, X))
            )
            value = jnp.where(outside, 0.0, value)
            if ze == 0:
                value = jnp.where(has_z[0], value, 0.0)
            if ze == Z + 1:
                value = jnp.where(has_z[1], value, 0.0)
            value = 0.125 * (from_left(value) + from_right(value)) + 0.25 * value
            flow[ze, comp] = 0.5 * value + 0.25 * (pltpu.roll(value, 1, axis=0) + pltpu.roll(value, 15, axis=0))
    for comp in range(3):
        for zs in range(Z + 4):
            value = None
            for ze, weight in ((zs - 2, 0.25), (zs - 1, 0.5), (zs, 0.25)):
                if 0 <= ze < Z + 2:
                    term = weight * flow[ze, comp]
                    value = term if value is None else value + term
            sm[0, zs, comp] = value[:Y]
            sm[1, zs, comp] = value[Y:]

    send_zr = [remote(zs_.at[t], zr.at[1 - t], 22 + t, z_of[t], gy) for t in range(2)]
    send_rz = [remote(sm.at[0, pl.ds((0, Z + 2)[t], 2)], rz.at[1 - t], 24 + t, z_of[t], gy) for t in range(2)]
    send_ry = [remote(ys.at[s], yr.at[1 - s], 26 + s, gz, y_of[s]) for s in range(2)]
    row = iota((Y, X), 0)
    low, high = row < 2, row >= Y - 2

    def moved(value, by):
        return pltpu.roll(value, by % Y, axis=0) if by % Y else value

    for t in range(2):
        for comp in range(3):
            a, b = sm[1, (0, Z + 2)[t], comp], sm[1, (0, Z + 2)[t] + 1, comp]
            kept = jnp.where(low, a, jnp.where(high, b, 0.0))
            zs_[t, comp] = kept + moved(jnp.where(high, a, jnp.where(low, b, 0.0)), 4)

        @pl.when(has_z[t])
        def _():
            send_zr[t].start()

    for side in range(2):
        @pl.when(jnp.logical_not(has_z[side]))
        def _():
            zr[side] = jnp.zeros((3, Y, X), F32)
            rz[side] = jnp.zeros((2, 3, Y, X), F32)

        @pl.when(jnp.logical_not(has_y[side]))
        def _():
            yr[side] = jnp.zeros((4 * Y, X), BF16)

    for side in range(2):
        @pl.when(has_z[side])
        def _():
            send_zr[1 - side].wait_recv()
    packs = [[], []]
    for comp in range(3):
        up, down = None, None
        for z in range(Z):
            value = zr[z // 2, comp]
            turned = moved(value, 4)
            if z % 2 == 0:
                value = jnp.where(low, value, turned)
            else:
                value = jnp.where(low, turned, value)
            value = sm[1, z + 2, comp] + value
            first = moved(jnp.where(low, value, 0.0), 2 * z)
            last = moved(jnp.where(high, value, 0.0), 2 * z + 2)
            up = first if up is None else up + first
            down = last if down is None else down + last
        packs[1].append(up)
        packs[0].append(down)
    for s in range(2):
        ys[s] = jnp.concatenate([*packs[s], jnp.zeros((Y, X), F32)], axis=0).astype(BF16)

        @pl.when(has_y[s])
        def _():
            send_ry[s].start()
    for t in range(2):
        @pl.when(has_z[t])
        def _():
            send_rz[t].start()

    for side in range(2):
        @pl.when(has_z[side])
        def _():
            send_rz[1 - side].wait_recv()
    for comp in range(3):
        for z in range(Z):
            sm[0, z + 2, comp] += rz[z // 2, z % 2, comp]
    for side in range(2):
        @pl.when(has_y[side])
        def _():
            send_ry[1 - side].wait_recv()
    came = [yr[s].astype(F32) for s in range(2)]
    for comp in range(3):
        for z in range(Z):
            first = moved(came[0][comp * Y : (comp + 1) * Y], -2 * z)
            last = moved(came[1][comp * Y : (comp + 1) * Y], -2 - 2 * z)
            value = jnp.where(low, first, jnp.where(high, last, 0.0))
            out[comp, z] = sm[0, z + 2, comp] + value

    for side in range(2):
        @pl.when(has_z[side])
        def _():
            send_slab[side].wait_send()
            send_zr[side].wait_send()
            send_rz[side].wait_send()

        @pl.when(far[side])
        def _():
            for z in range(K):
                send_way[side][z].wait_send()
            for z in range(K, Z):
                send_y[side][z].wait_send()

        @pl.when(has_y[side] & jnp.logical_not(far[side]))
        def _():
            for z in range(Z):
                send_y[side][z].wait_send()

        @pl.when(helps[side])
        def _():
            for z in range(K):
                pass_on[side][z].wait_send()

        @pl.when(has_y[side])
        def _():
            send_ry[side].wait_send()

        for s in range(2):
            @pl.when(has_z[side] & has_y[s])
            def _():
                send_corner[side][s].wait_send()


def block(features, s1, t1, w1, b1, s2, t2, w2, b2, fw):
    def row(v):
        return v.reshape(1, C)

    vm = pltpu.VMEM
    dma = pltpu.SemaphoreType.DMA
    return pl.pallas_call(
        kernel,
        out_shape=pltpu.VMEM((3, Z, Y, X), F32),
        in_specs=[pl.BlockSpec(memory_space=pltpu.HBM)] * 10,
        out_specs=pl.BlockSpec(memory_space=pltpu.VMEM),
        scratch_shapes=[
            vm((C, Z, Y, X), BF16),
            vm((6, 1, C), F32),
            vm((3, 3, C, C), BF16),
            vm((3, 3, C, C), BF16),
            vm((2, C), BF16),
            vm((Z, R, X), BF16),
            vm((Z + 2, 3, R, X), BF16),
            vm((Z, 2, C, X), BF16),
            vm((2, 2, C, X), BF16),
            vm((Z + 2, 2, C, X), BF16),
            vm((4, R, 128), F32),
            vm((2, 2 * C, 128), F32),
            vm((R, 3 * R), BF16),
            vm((3, R, 3 * R), BF16),
            vm((3, R, R), BF16),
            vm((2 * C, 3 * R), BF16),
            vm((3, 2 * C, R), BF16),
            vm((2 * C, 6 * C), BF16),
            vm((2 * C, 6 * C), BF16),
            vm((192, R), BF16),
            vm((288, R), BF16),
            vm((192, R), BF16),
            vm((192, 2 * C), BF16),
            vm((192, 2 * C), BF16),
            vm((16, R), BF16),
            vm((2, Z, R, X), F32),
            vm((2, Z, 2 * C, X), F32),
            vm((3, Z + 2, 3, 2, Y, X), F32),
            vm((2, Z + 4, 3, Y, X), F32),
            vm((2, Z - 1, C, X), BF16),
            vm((2, 3, Y, X), F32),
            vm((2, 3, Y, X), F32),
            vm((2, 2, 3, Y, X), F32),
            vm((2, 4 * Y, X), BF16),
            vm((2, 4 * Y, X), BF16),
            dma((Z + 9,)),
            dma((34,)),
            dma((34,)),
        ],
        compiler_params=pltpu.CompilerParams(
            collective_id=0, has_side_effects=True, vmem_limit_bytes=48 * 1024 * 1024
        ),
    )(*[pltpu.with_memory_space_constraint(v, pltpu.HBM) for v in (features, row(s1), row(t1), w1, row(b1), row(s2), row(t2), w2, row(b2), fw)])


def solution(mesh):
    return jax.shard_map(
        block,
        mesh=mesh,
        in_specs=(P(None, "gz", "gy", None), P(), P(), P(), P(), P(), P(), P(), P(), P()),
        out_specs=P(None, "gz", "gy", None),
        check_vma=False,
    )
```

```python
import jax
import jax.numpy as jnp
from jax import lax
from jax.experimental import pallas as pl
from jax.experimental.pallas import tpu as pltpu
from jax.sharding import PartitionSpec as P

MESH = pl.DeviceIdType.MESH
F32 = jnp.float32
BF16 = jnp.bfloat16
C = 32
Z = 4
Y = 8
X = 256
R = C * Y
K = 3
NEAR = 2
G = 4


def iota(shape, dim):
    return lax.broadcasted_iota(jnp.int32, shape, dim)


def dot(a, b):
    return jnp.dot(a, b, preferred_element_type=F32)


def one_hot(flags):
    return jnp.where(flags, 1.0, 0.0).astype(BF16)


def from_left(value):
    moved = pltpu.roll(value, 1, axis=1)
    return jnp.where(iota(value.shape, 1) == 0, 0.0, moved)


def from_right(value):
    last = value.shape[1] - 1
    moved = pltpu.roll(value, last, axis=1)
    return jnp.where(iota(value.shape, 1) == last, 0.0, moved)


def kernel(
    x_hbm, s1_hbm, t1_hbm, w1_hbm, b1_hbm, s2_hbm, t2_hbm, w2_hbm, b2_hbm, fw_hbm,
    out,
    xin, par, w1, w2, fw, raw, ux, edge, ez, halo,
    cols, cols_e, wxy, wxz, wyz, wxy_e, wyz_e, whx, why, bxy, bxz, byz, bxy_e, byz_e, fres,
    hid, hid_e, acc, sm,
    rel, zs_, zr, rz, ys, yr,
    lsem, ssem, rsem,
):
    gz, gy = lax.axis_index("gz"), lax.axis_index("gy")
    nz, ny = lax.axis_size("gz"), lax.axis_size("gy")
    has_z = (gz > 0, gz < nz - 1)
    has_y = (gy > 0, gy < ny - 1)
    z_of = (gz - 1, gz + 1)
    y_of = (gy - 1, gy + 1)
    place = gy % G
    far = (has_y[0] & (place == 0), has_y[1] & (place == G - 1))
    way = (gy + G - 1, gy - G + 1)
    helps = ((place == G - 1) & (gy >= G), (place == 0) & (gy + G < ny))
    source = (gy - G + 1, gy + G - 1)
    beyond_group = (gy - G, gy + G)
    near_way = (gy + 1, gy - 1)
    near_helps = ((place == 1) & (gy >= G), (place == G - 2) & (gy + 2 < ny))
    near_beyond = (gy - 2, gy + 2)

    barrier = pltpu.get_barrier_semaphore()
    for side in range(2):
        @pl.when(has_z[side])
        def _():
            pl.semaphore_signal(barrier, inc=1, device_id=(z_of[side], gy), device_id_type=MESH)

        @pl.when(has_y[side])
        def _():
            pl.semaphore_signal(barrier, inc=1, device_id=(gz, y_of[side]), device_id_type=MESH)

        @pl.when(helps[side])
        def _():
            pl.semaphore_signal(barrier, inc=1, device_id=(gz, source[side]), device_id_type=MESH)

    order = (0, 3, 1, 2)
    loads = {z: pltpu.make_async_copy(x_hbm.at[:, z], xin.at[:, z], lsem.at[z]) for z in order}
    params = [
        pltpu.make_async_copy(source, par.at[i], lsem.at[Z + i])
        for i, source in enumerate((s1_hbm, t1_hbm, b1_hbm, s2_hbm, t2_hbm, b2_hbm))
    ]
    weights = [
        pltpu.make_async_copy(source, target, lsem.at[Z + 6 + i])
        for i, (source, target) in enumerate(((w1_hbm, w1), (w2_hbm, w2), (fw_hbm, fw)))
    ]
    for copy in (*params, loads[0], loads[3], loads[1], loads[2], *weights):
        copy.start()

    for side in range(2):
        slot = (0, Z + 1)[side]

        @pl.when(jnp.logical_not(has_z[side]))
        def _():
            ux[slot, 1] = jnp.zeros((R, X), BF16)
            halo[slot] = jnp.zeros((2, C, X), BF16)

        @pl.when(jnp.logical_not(has_y[side]))
        def _():
            for ze in range(1, Z + 1):
                halo[ze, side] = jnp.zeros((C, X), BF16)

        for yside in range(2):
            @pl.when(has_z[side] & jnp.logical_not(has_y[yside]))
            def _():
                halo[slot, yside] = jnp.zeros((C, X), BF16)

    for copy in params:
        copy.wait()
    pick = iota((R, C), 0) // Y == iota((R, C), 1)

    def column(row):
        return jnp.sum(jnp.where(pick, row, 0.0), axis=1, keepdims=True)

    b1_row, s2_row, t2_row, b2_row = par[2], par[3], par[4], par[5]
    cols[0] = jnp.broadcast_to(column(par[0]), (R, 128))
    cols[1] = jnp.broadcast_to(column(par[1]), (R, 128))
    cols[2] = jnp.broadcast_to(column(s2_row), (R, 128))
    cols[3] = jnp.broadcast_to(column(b1_row * s2_row + t2_row), (R, 128))

    pick_e = iota((2 * C, C), 0) % C == iota((2 * C, C), 1)
    cols_e[0] = jnp.broadcast_to(
        jnp.sum(jnp.where(pick_e, s2_row, 0.0), axis=1, keepdims=True), (2 * C, 128)
    )
    cols_e[1] = jnp.broadcast_to(
        jnp.sum(jnp.where(pick_e, b1_row * s2_row + t2_row, 0.0), axis=1, keepdims=True), (2 * C, 128)
    )

    def wide(half):
        return jnp.concatenate([half, half], axis=1)

    rows, lanes = iota((2 * C, R), 0), iota((2 * C, R), 1)
    edge_pick = one_hot(lanes == (rows % C) * Y + (rows // C) * (Y - 1))
    for z in order:
        loads[z].wait()
        value = xin[:, z].astype(F32).reshape(R, X)
        raw[z] = value.astype(BF16)
        unit = jnp.maximum(value * wide(cols[0]) + wide(cols[1]), 0.0).astype(BF16)
        ux[z + 1, 1] = unit
        edge[z] = dot(edge_pick, unit).astype(BF16).reshape(2, C, X)

    def remote(source, target, i, zi, yi):
        return pltpu.make_async_remote_copy(
            src_ref=source, dst_ref=target, send_sem=ssem.at[i], recv_sem=rsem.at[i],
            device_id=(zi, yi), device_id_type=MESH,
        )

    send_ez = [remote(edge.at[(0, Z - 1)[s]], ez.at[1 - s], s, z_of[s], gy) for s in range(2)]
    send_slab = [
        remote(ux.at[(1, Z)[s], 1], ux.at[(Z + 1, 0)[s], 1], 2 + s, z_of[s], gy) for s in range(2)
    ]
    send_y = [
        [remote(edge.at[z, s], halo.at[z + 1, 1 - s], 4 + s * Z + z, gz, y_of[s]) for z in range(Z)]
        for s in range(2)
    ]
    send_way = [
        [remote(edge.at[z, s], rel.at[s, z], 16 + s * (Z - 1) + z, gz, (way if z < NEAR else near_way)[s]) for z in range(K)]
        for s in range(2)
    ]
    pass_on = [
        [
            pltpu.make_async_remote_copy(
                src_ref=rel.at[s, z], dst_ref=halo.at[z + 1, 1 - s], send_sem=ssem.at[28 + s * (Z - 1) + z],
                recv_sem=rsem.at[4 + s * Z + z], device_id=(gz, (beyond_group if z < NEAR else near_beyond)[s]), device_id_type=MESH,
            )
            for z in range(K)
        ]
        for s in range(2)
    ]
    send_corner = [
        [
            remote(ez.at[zs, ys_], halo.at[(0, Z + 1)[zs], 1 - ys_], 12 + 2 * zs + ys_, gz, y_of[ys_])
            for ys_ in range(2)
        ]
        for zs in range(2)
    ]

    def relay(s):
        for flag, rows in ((helps[s], range(NEAR)), (near_helps[s], range(NEAR, K))):
            @pl.when(flag)
            def _():
                for z in rows:
                    send_way[s][z].wait_recv()
                    pass_on[s][z].start()

    for copy in weights:
        copy.wait()
    spread = one_hot(iota((C, R), 1) // Y == iota((C, R), 0))
    repeat = one_hot(pick)
    wide_w1 = dot(w1[...].reshape(9 * C, C), spread).astype(BF16)
    shift = iota((R, R), 1) % Y - iota((R, R), 0) % Y
    for j in range(3):
        banded = None
        for i in range(3):
            k = 3 * i + j
            full = dot(repeat, wide_w1[k * C : (k + 1) * C])
            term = jnp.where(shift == i - 1, full, 0.0)
            banded = term if banded is None else banded + term
            wxz[i, :, j * R : (j + 1) * R] = jnp.where(shift == 0, full, 0.0).astype(BF16)
        wxy[:, j * R : (j + 1) * R] = banded.astype(BF16)
    for i in range(3):
        banded = None
        for j in range(3):
            k = 3 * i + j
            full = dot(repeat, wide_w1[k * C : (k + 1) * C])
            term = jnp.where(shift == j - 1, full, 0.0)
            banded = term if banded is None else banded + term
        wyz[i] = banded.astype(BF16)
    for i in range(3):
        wyz_e[i] = dot(edge_pick, wyz[i]).astype(BF16)
    wxy_e[...] = dot(edge_pick, wxy[...]).astype(BF16)
    reach = 6 * C
    touched = iota((2 * C, reach), 0) // C == (iota((2 * C, reach), 1) // C) % 2
    repeat_e = one_hot(pick_e)
    packed_x = jnp.zeros((C, reach), F32)
    packed_y = jnp.zeros((C, reach), F32)
    for tap in range(3):
        for side in range(2):
            put = one_hot(iota((C, reach), 1) == iota((C, reach), 0) + (2 * tap + side) * C)
            packed_x += dot(w1[2 * side, tap], put)
            packed_y += dot(w1[tap, 2 * side], put)
    whx[...] = jnp.where(touched, dot(repeat_e, packed_x.astype(BF16)), 0.0).astype(BF16)
    why[...] = jnp.where(touched, dot(repeat_e, packed_y.astype(BF16)), 0.0).astype(BF16)

    rows, lanes = iota((2 * 16, R), 0) % 16, iota((2 * 16, R), 1) % Y
    first = jnp.broadcast_to(fw[0:1, :].astype(F32), (16, C))
    second = jnp.broadcast_to(fw[1:2, :].astype(F32), (16, C))
    fw32 = jnp.concatenate([first, second], axis=0)
    fw16 = jnp.concatenate([first[:Y], second[:Y]], axis=0)
    highs, lows = [], []
    for i in range(3):
        for j in range(3):
            g = dot(fw32.astype(BF16), w2[i, j])
            high = g.astype(BF16)
            highs.append(high)
            lows.append((g - high.astype(F32)).astype(BF16))
    taps = dot(jnp.concatenate(highs + lows, axis=0), spread).reshape(2, 3, 3, 32, R)
    same = rows == lanes
    for part in range(2):
        for a in range(3):
            band_xy = jnp.zeros((32, R), F32)
            band_yz = jnp.zeros((32, R), F32)
            for b in range(3):
                hit = rows == (lanes + (17 - b)) % 16
                band_xy += jnp.where(hit, taps[part, b, a], 0.0)
                band_yz += jnp.where(hit, taps[part, a, b], 0.0)
            at = (part * 3 + a) * 32
            bxy[at : at + 32, :] = band_xy.astype(BF16)
            byz[at : at + 32, :] = band_yz.astype(BF16)
        for i in range(3):
            for j in range(3):
                value = jnp.where(same, taps[part, i, j], 0.0)
                at = (part * 9 + i * 3 + j) * 16
                bxz[at : at + 16, :] = jnp.concatenate([value[:Y], value[16 : 16 + Y]], axis=0).astype(BF16)
    rows, lanes = iota((R, 2 * C), 0), iota((R, 2 * C), 1)
    edge_put = one_hot(rows == (lanes % C) * Y + (lanes // C) * (Y - 1))
    bxy_e[...] = dot(bxy[...], edge_put).astype(BF16)
    byz_e[...] = dot(byz[...], edge_put).astype(BF16)
    own = iota((16, R), 0) % Y == iota((16, R), 1) % Y
    fres[...] = jnp.where(own, dot(fw16.astype(BF16), spread), 0.0).astype(BF16)
    bias = jnp.sum(fw16 * b2_row, axis=1, keepdims=True)

    peers = sum(flag.astype(jnp.int32) for flag in (*has_z, *has_y, *far))
    pl.semaphore_wait(barrier, peers)

    for side in range(2):
        @pl.when(has_z[side])
        def _():
            send_ez[side].start()
    for side in range(2):
        @pl.when(far[side])
        def _():
            for z in range(K):
                send_way[side][z].start()
            for z in range(K, Z):
                send_y[side][z].start()

        @pl.when(has_y[side] & jnp.logical_not(far[side]))
        def _():
            for z in range(Z):
                send_y[side][z].start()
    for side in range(2):
        @pl.when(has_z[side])
        def _():
            send_slab[side].start()

    def shifted(ze):
        value = ux[ze, 1].astype(F32)
        ux[ze, 0] = from_left(value).astype(BF16)
        ux[ze, 2] = from_right(value).astype(BF16)

    for ze in range(1, Z + 1):
        shifted(ze)

    row8 = iota((R, X), 0) % Y
    inner = (row8 > 0) & (row8 < Y - 1)

    def active(hidden):
        return jnp.maximum(hidden * wide(cols[2]) + wide(cols[3]), 0.0)

    def active_e(hidden):
        return jnp.maximum(hidden * wide(cols_e[0]) + wide(cols_e[1]), 0.0).astype(BF16)

    def add_xy(z, both):
        part = (both[:96] + both[96:]).reshape(3, 2, 2, Y, X)
        for j in range(3):
            acc[j, z + 1, 1] += part[j, 0]
            acc[j, z + 1, 2] += part[j, 1]

    def add_yz(z, both):
        part = (both[:96] + both[96:]).reshape(3, 2, 2, Y, X)
        for i in range(3):
            acc[1, z + 2 - i, 0] += part[i, 0]
            acc[1, z + 2 - i, 1] += part[i, 1]

    acc[...] = jnp.zeros_like(acc)
    relay(0)
    for z in range(Z):
        wide_x = ux[z + 1].reshape(3 * R, X)
        hid_e[0, z] = dot(wxy_e[...], wide_x)
        value = jnp.where(inner, active(dot(wxy[...], wide_x)), 0.0).astype(BF16)
        add_xy(z, dot(bxy[...], value))

    for side in range(2):
        @pl.when(has_z[side])
        def _():
            send_ez[side].wait_send()
            send_ez[1 - side].wait_recv()
            for yside in range(2):
                @pl.when(has_y[yside])
                def _():
                    send_corner[side][yside].start()

    for z in range(Z):
        xz = dot(wxz[1], ux[z + 1].reshape(3 * R, X))
        yz = dot(wyz[1], ux[z + 1, 1])
        yz_e = dot(wyz_e[1], ux[z + 1, 1])
        for i in (0, 2):
            if 1 <= z + i <= Z:
                xz += dot(wxz[i], ux[z + i].reshape(3 * R, X))
                yz += dot(wyz[i], ux[z + i, 1])
                yz_e += dot(wyz_e[i], ux[z + i, 1])
        hid[0, z] = xz
        hid[1, z] = yz
        hid_e[1, z] = yz_e
        residual = dot(fres[...], raw[z]) + bias
        r0, r1 = residual[:Y], residual[Y:]
        acc[1, z + 1, 0, 0] += 2.0 * r0
        acc[1, z + 1, 1, 0] += r0 + r1
        acc[1, z + 1, 2, 0] += 2.0 * r1

    def finish(z):
        both = dot(bxz[...], active(hid[0, z]).astype(BF16))
        part = both[:144] + both[144:]
        for i in range(3):
            for j in range(3):
                at = (i * 3 + j) * 16
                acc[j, z + 2 - i, 0, 0] += part[at : at + Y]
                acc[j, z + 2 - i, 2, 0] += part[at + Y : at + 16]
        add_yz(z, dot(byz[...], jnp.where(inner, active(hid[1, z]), 0.0).astype(BF16)))

    for z in range(1, Z - 1):
        finish(z)

    relay(1)

    for side in range(2):
        @pl.when(has_z[side])
        def _():
            send_slab[1 - side].wait_recv()
    for ze in (0, Z + 1):
        shifted(ze)
    for z, i in ((0, 0), (Z - 1, 2)):
        hid[0, z] += dot(wxz[i], ux[z + i].reshape(3 * R, X))
        hid[1, z] += dot(wyz[i], ux[z + i, 1])
        hid_e[1, z] += dot(wyz_e[i], ux[z + i, 1])
        finish(z)

    for side in range(2):
        @pl.when(has_y[side])
        def _():
            for z in range(Z):
                send_y[1 - side][z].wait_recv()
    hidden = []
    for z in range(Z):
        beside = halo[z + 1].reshape(2 * C, X)
        wider = beside.astype(F32)
        three = jnp.concatenate([from_left(wider).astype(BF16), beside, from_right(wider).astype(BF16)], axis=0)
        hidden.append(hid_e[0, z] + dot(whx[...], three))
    both = [dot(bxy_e[...], active_e(value)) for value in hidden]
    for z in range(Z):
        add_xy(z, both[z])
    for side in range(2):
        @pl.when(has_y[side])
        def _():
            for zside in range(2):
                @pl.when(has_z[zside])
                def _():
                    send_corner[zside][1 - side].wait_recv()
    hidden = [hid_e[1, z] + dot(why[...], halo[z : z + 3].reshape(6 * C, X)) for z in range(Z)]
    both = [dot(byz_e[...], active_e(value)) for value in hidden]
    for z in range(Z):
        add_yz(z, both[z])

    rows16x = iota((16, X), 0)
    outside = ((rows16x == 15) & jnp.logical_not(has_y[0])) | ((rows16x == Y) & jnp.logical_not(has_y[1]))
    flow = {}
    for ze in range(Z + 2):
        for comp in range(3):
            value = (
                from_left(acc[0, ze, comp].reshape(16, X))
                + acc[1, ze, comp].reshape(16, X)
                + from_right(acc[2, ze, comp].reshape(16, X))
            )
            value = jnp.where(outside, 0.0, value)
            if ze == 0:
                value = jnp.where(has_z[0], value, 0.0)
            if ze == Z + 1:
                value = jnp.where(has_z[1], value, 0.0)
            value = 0.125 * (from_left(value) + from_right(value)) + 0.25 * value
            flow[ze, comp] = 0.5 * value + 0.25 * (pltpu.roll(value, 1, axis=0) + pltpu.roll(value, 15, axis=0))
    for comp in range(3):
        for zs in range(Z + 4):
            value = None
            for ze, weight in ((zs - 2, 0.25), (zs - 1, 0.5), (zs, 0.25)):
                if 0 <= ze < Z + 2:
                    term = weight * flow[ze, comp]
                    value = term if value is None else value + term
            sm[0, zs, comp] = value[:Y]
            sm[1, zs, comp] = value[Y:]

    send_zr = [remote(zs_.at[t], zr.at[1 - t], 22 + t, z_of[t], gy) for t in range(2)]
    send_rz = [remote(sm.at[0, pl.ds((0, Z + 2)[t], 2)], rz.at[1 - t], 24 + t, z_of[t], gy) for t in range(2)]
    send_ry = [remote(ys.at[s], yr.at[1 - s], 26 + s, gz, y_of[s]) for s in range(2)]
    row = iota((Y, X), 0)
    low, high = row < 2, row >= Y - 2

    def moved(value, by):
        return pltpu.roll(value, by % Y, axis=0) if by % Y else value

    for t in range(2):
        for comp in range(3):
            a, b = sm[1, (0, Z + 2)[t], comp], sm[1, (0, Z + 2)[t] + 1, comp]
            kept = jnp.where(low, a, jnp.where(high, b, 0.0))
            zs_[t, comp] = kept + moved(jnp.where(high, a, jnp.where(low, b, 0.0)), 4)

        @pl.when(has_z[t])
        def _():
            send_zr[t].start()

    for side in range(2):
        @pl.when(jnp.logical_not(has_z[side]))
        def _():
            zr[side] = jnp.zeros((3, Y, X), F32)
            rz[side] = jnp.zeros((2, 3, Y, X), F32)

        @pl.when(jnp.logical_not(has_y[side]))
        def _():
            yr[side] = jnp.zeros((4 * Y, X), BF16)

    for side in range(2):
        @pl.when(has_z[side])
        def _():
            send_zr[1 - side].wait_recv()
    packs = [[], []]
    for comp in range(3):
        up, down = None, None
        for z in range(Z):
            value = zr[z // 2, comp]
            turned = moved(value, 4)
            if z % 2 == 0:
                value = jnp.where(low, value, turned)
            else:
                value = jnp.where(low, turned, value)
            value = sm[1, z + 2, comp] + value
            first = moved(jnp.where(low, value, 0.0), 2 * z)
            last = moved(jnp.where(high, value, 0.0), 2 * z + 2)
            up = first if up is None else up + first
            down = last if down is None else down + last
        packs[1].append(up)
        packs[0].append(down)
    for s in range(2):
        ys[s] = jnp.concatenate([*packs[s], jnp.zeros((Y, X), F32)], axis=0).astype(BF16)

        @pl.when(has_y[s])
        def _():
            send_ry[s].start()
    for t in range(2):
        @pl.when(has_z[t])
        def _():
            send_rz[t].start()

    for side in range(2):
        @pl.when(has_z[side])
        def _():
            send_rz[1 - side].wait_recv()
    for comp in range(3):
        for z in range(Z):
            sm[0, z + 2, comp] += rz[z // 2, z % 2, comp]
    for side in range(2):
        @pl.when(has_y[side])
        def _():
            send_ry[1 - side].wait_recv()
    came = [yr[s].astype(F32) for s in range(2)]
    for comp in range(3):
        for z in range(Z):
            first = moved(came[0][comp * Y : (comp + 1) * Y], -2 * z)
            last = moved(came[1][comp * Y : (comp + 1) * Y], -2 - 2 * z)
            value = jnp.where(low, first, jnp.where(high, last, 0.0))
            out[comp, z] = sm[0, z + 2, comp] + value

    for side in range(2):
        @pl.when(has_z[side])
        def _():
            send_slab[side].wait_send()
            send_zr[side].wait_send()
            send_rz[side].wait_send()

        @pl.when(far[side])
        def _():
            for z in range(K):
                send_way[side][z].wait_send()
            for z in range(K, Z):
                send_y[side][z].wait_send()

        @pl.when(has_y[side] & jnp.logical_not(far[side]))
        def _():
            for z in range(Z):
                send_y[side][z].wait_send()

        for flag, rows in ((helps[side], range(NEAR)), (near_helps[side], range(NEAR, K))):
            @pl.when(flag)
            def _():
                for z in rows:
                    pass_on[side][z].wait_send()

        @pl.when(has_y[side])
        def _():
            send_ry[side].wait_send()

        for s in range(2):
            @pl.when(has_z[side] & has_y[s])
            def _():
                send_corner[side][s].wait_send()


def block(features, s1, t1, w1, b1, s2, t2, w2, b2, fw):
    def row(v):
        return v.reshape(1, C)

    vm = pltpu.VMEM
    dma = pltpu.SemaphoreType.DMA
    return pl.pallas_call(
        kernel,
        out_shape=pltpu.VMEM((3, Z, Y, X), F32),
        in_specs=[pl.BlockSpec(memory_space=pltpu.HBM)] * 10,
        out_specs=pl.BlockSpec(memory_space=pltpu.VMEM),
        scratch_shapes=[
            vm((C, Z, Y, X), BF16),
            vm((6, 1, C), F32),
            vm((3, 3, C, C), BF16),
            vm((3, 3, C, C), BF16),
            vm((2, C), BF16),
            vm((Z, R, X), BF16),
            vm((Z + 2, 3, R, X), BF16),
            vm((Z, 2, C, X), BF16),
            vm((2, 2, C, X), BF16),
            vm((Z + 2, 2, C, X), BF16),
            vm((4, R, 128), F32),
            vm((2, 2 * C, 128), F32),
            vm((R, 3 * R), BF16),
            vm((3, R, 3 * R), BF16),
            vm((3, R, R), BF16),
            vm((2 * C, 3 * R), BF16),
            vm((3, 2 * C, R), BF16),
            vm((2 * C, 6 * C), BF16),
            vm((2 * C, 6 * C), BF16),
            vm((192, R), BF16),
            vm((288, R), BF16),
            vm((192, R), BF16),
            vm((192, 2 * C), BF16),
            vm((192, 2 * C), BF16),
            vm((16, R), BF16),
            vm((2, Z, R, X), F32),
            vm((2, Z, 2 * C, X), F32),
            vm((3, Z + 2, 3, 2, Y, X), F32),
            vm((2, Z + 4, 3, Y, X), F32),
            vm((2, Z - 1, C, X), BF16),
            vm((2, 3, Y, X), F32),
            vm((2, 3, Y, X), F32),
            vm((2, 2, 3, Y, X), F32),
            vm((2, 4 * Y, X), BF16),
            vm((2, 4 * Y, X), BF16),
            dma((Z + 9,)),
            dma((34,)),
            dma((34,)),
        ],
        compiler_params=pltpu.CompilerParams(
            collective_id=0, has_side_effects=True, vmem_limit_bytes=48 * 1024 * 1024
        ),
    )(*[pltpu.with_memory_space_constraint(v, pltpu.HBM) for v in (features, row(s1), row(t1), w1, row(b1), row(s2), row(t2), w2, row(b2), fw)])


def solution(mesh):
    return jax.shard_map(
        block,
        mesh=mesh,
        in_specs=(P(None, "gz", "gy", None), P(), P(), P(), P(), P(), P(), P(), P(), P()),
        out_specs=P(None, "gz", "gy", None),
        check_vma=False,
    )
```

```python
import jax
import jax.numpy as jnp
from jax import lax
from jax.experimental import pallas as pl
from jax.experimental.pallas import tpu as pltpu
from jax.sharding import PartitionSpec as P

MESH = pl.DeviceIdType.MESH
F32 = jnp.float32
BF16 = jnp.bfloat16
C = 32
Z = 4
Y = 8
X = 256
R = C * Y
K = 3
NEAR = 2
G = 4


def iota(shape, dim):
    return lax.broadcasted_iota(jnp.int32, shape, dim)


def dot(a, b):
    return jnp.dot(a, b, preferred_element_type=F32)


def one_hot(flags):
    return jnp.where(flags, 1.0, 0.0).astype(BF16)


def from_left(value):
    moved = pltpu.roll(value, 1, axis=1)
    return jnp.where(iota(value.shape, 1) == 0, 0.0, moved)


def from_right(value):
    last = value.shape[1] - 1
    moved = pltpu.roll(value, last, axis=1)
    return jnp.where(iota(value.shape, 1) == last, 0.0, moved)


def kernel(
    x_hbm, s1_hbm, t1_hbm, w1_hbm, b1_hbm, s2_hbm, t2_hbm, w2_hbm, b2_hbm, fw_hbm,
    out,
    xin, par, w1, w2, fw, raw, ux, edge, ez, halo,
    cols, cols_e, wxy, wxz, wyz, wxy_e, wyz_e, whx, why, bxy, bxz, byz, bxy_e, byz_e, fres,
    hid, hid_e, acc, sm,
    rel, zs_, zr, rz, ys, yr,
    lsem, ssem, rsem,
):
    gz, gy = lax.axis_index("gz"), lax.axis_index("gy")
    nz, ny = lax.axis_size("gz"), lax.axis_size("gy")
    has_z = (gz > 0, gz < nz - 1)
    has_y = (gy > 0, gy < ny - 1)
    z_of = (gz - 1, gz + 1)
    y_of = (gy - 1, gy + 1)
    place = gy % G
    far = (has_y[0] & (place == 0), has_y[1] & (place == G - 1))
    way = (gy + G - 1, gy - G + 1)
    helps = ((place == G - 1) & (gy >= G), (place == 0) & (gy + G < ny))
    source = (gy - G + 1, gy + G - 1)
    beyond_group = (gy - G, gy + G)
    near_way = (gy + 1, gy - 1)
    near_helps = ((place == 1) & (gy >= G), (place == G - 2) & (gy + 2 < ny))
    near_beyond = (gy - 2, gy + 2)

    barrier = pltpu.get_barrier_semaphore()
    for side in range(2):
        @pl.when(has_z[side])
        def _():
            pl.semaphore_signal(barrier, inc=1, device_id=(z_of[side], gy), device_id_type=MESH)

        @pl.when(has_y[side])
        def _():
            pl.semaphore_signal(barrier, inc=1, device_id=(gz, y_of[side]), device_id_type=MESH)

        @pl.when(helps[side])
        def _():
            pl.semaphore_signal(barrier, inc=1, device_id=(gz, source[side]), device_id_type=MESH)

    order = (0, 3, 1, 2)
    loads = {z: pltpu.make_async_copy(x_hbm.at[:, z], xin.at[:, z], lsem.at[z]) for z in order}
    params = [
        pltpu.make_async_copy(source, par.at[i], lsem.at[Z + i])
        for i, source in enumerate((s1_hbm, t1_hbm, b1_hbm, s2_hbm, t2_hbm, b2_hbm))
    ]
    weights = [
        pltpu.make_async_copy(source, target, lsem.at[Z + 6 + i])
        for i, (source, target) in enumerate(((w1_hbm, w1), (w2_hbm, w2), (fw_hbm, fw)))
    ]
    for copy in (*params, loads[0], loads[3], loads[1], loads[2], *weights):
        copy.start()

    for side in range(2):
        slot = (0, Z + 1)[side]

        @pl.when(jnp.logical_not(has_z[side]))
        def _():
            ux[slot, 1] = jnp.zeros((R, X), BF16)
            halo[slot] = jnp.zeros((2, C, X), BF16)

        @pl.when(jnp.logical_not(has_y[side]))
        def _():
            for ze in range(1, Z + 1):
                halo[ze, side] = jnp.zeros((C, X), BF16)

        for yside in range(2):
            @pl.when(has_z[side] & jnp.logical_not(has_y[yside]))
            def _():
                halo[slot, yside] = jnp.zeros((C, X), BF16)

    for copy in params:
        copy.wait()
    pick = iota((R, C), 0) // Y == iota((R, C), 1)

    def column(row):
        return jnp.sum(jnp.where(pick, row, 0.0), axis=1, keepdims=True)

    b1_row, s2_row, t2_row, b2_row = par[2], par[3], par[4], par[5]
    cols[0] = jnp.broadcast_to(column(par[0]), (R, 128))
    cols[1] = jnp.broadcast_to(column(par[1]), (R, 128))
    cols[2] = jnp.broadcast_to(column(s2_row), (R, 128))
    cols[3] = jnp.broadcast_to(column(b1_row * s2_row + t2_row), (R, 128))

    pick_e = iota((2 * C, C), 0) % C == iota((2 * C, C), 1)
    cols_e[0] = jnp.broadcast_to(
        jnp.sum(jnp.where(pick_e, s2_row, 0.0), axis=1, keepdims=True), (2 * C, 128)
    )
    cols_e[1] = jnp.broadcast_to(
        jnp.sum(jnp.where(pick_e, b1_row * s2_row + t2_row, 0.0), axis=1, keepdims=True), (2 * C, 128)
    )

    def wide(half):
        return jnp.concatenate([half, half], axis=1)

    rows, lanes = iota((2 * C, R), 0), iota((2 * C, R), 1)
    edge_pick = one_hot(lanes == (rows % C) * Y + (rows // C) * (Y - 1))
    for z in order:
        loads[z].wait()
        value = xin[:, z].astype(F32).reshape(R, X)
        raw[z] = value.astype(BF16)
        unit = jnp.maximum(value * wide(cols[0]) + wide(cols[1]), 0.0).astype(BF16)
        ux[z + 1, 1] = unit
        edge[z] = dot(edge_pick, unit).astype(BF16).reshape(2, C, X)

    def remote(source, target, i, zi, yi):
        return pltpu.make_async_remote_copy(
            src_ref=source, dst_ref=target, send_sem=ssem.at[i], recv_sem=rsem.at[i],
            device_id=(zi, yi), device_id_type=MESH,
        )

    send_ez = [remote(edge.at[(0, Z - 1)[s]], ez.at[1 - s], s, z_of[s], gy) for s in range(2)]
    send_slab = [
        remote(ux.at[(1, Z)[s], 1], ux.at[(Z + 1, 0)[s], 1], 2 + s, z_of[s], gy) for s in range(2)
    ]
    send_y = [
        [remote(edge.at[z, s], halo.at[z + 1, 1 - s], 4 + s * Z + z, gz, y_of[s]) for z in range(Z)]
        for s in range(2)
    ]
    send_way = [
        [remote(edge.at[z, s], rel.at[s, z], 16 + s * (Z - 1) + z, gz, (way if z < NEAR else near_way)[s]) for z in range(K)]
        for s in range(2)
    ]
    pass_on = [
        [
            pltpu.make_async_remote_copy(
                src_ref=rel.at[s, z], dst_ref=halo.at[z + 1, 1 - s], send_sem=ssem.at[28 + s * (Z - 1) + z],
                recv_sem=rsem.at[4 + s * Z + z], device_id=(gz, (beyond_group if z < NEAR else near_beyond)[s]), device_id_type=MESH,
            )
            for z in range(K)
        ]
        for s in range(2)
    ]
    send_corner = [
        [
            remote(ez.at[zs, ys_], halo.at[(0, Z + 1)[zs], 1 - ys_], 12 + 2 * zs + ys_, gz, y_of[ys_])
            for ys_ in range(2)
        ]
        for zs in range(2)
    ]

    def relay(s):
        for flag, rows in ((helps[s], range(NEAR)), (near_helps[s], range(NEAR, K))):
            @pl.when(flag)
            def _():
                for z in rows:
                    send_way[s][z].wait_recv()
                    pass_on[s][z].start()

    for copy in weights:
        copy.wait()
    spread = one_hot(iota((C, R), 1) // Y == iota((C, R), 0))
    repeat = one_hot(pick)
    wide_w1 = dot(w1[...].reshape(9 * C, C), spread).astype(BF16)
    shift = iota((R, R), 1) % Y - iota((R, R), 0) % Y
    for j in range(3):
        banded = None
        for i in range(3):
            k = 3 * i + j
            full = dot(repeat, wide_w1[k * C : (k + 1) * C])
            term = jnp.where(shift == i - 1, full, 0.0)
            banded = term if banded is None else banded + term
            wxz[i, :, j * R : (j + 1) * R] = jnp.where(shift == 0, full, 0.0).astype(BF16)
        wxy[:, j * R : (j + 1) * R] = banded.astype(BF16)
    for i in range(3):
        banded = None
        for j in range(3):
            k = 3 * i + j
            full = dot(repeat, wide_w1[k * C : (k + 1) * C])
            term = jnp.where(shift == j - 1, full, 0.0)
            banded = term if banded is None else banded + term
        wyz[i] = banded.astype(BF16)
    for i in range(3):
        wyz_e[i] = dot(edge_pick, wyz[i]).astype(BF16)
    wxy_e[...] = dot(edge_pick, wxy[...]).astype(BF16)
    reach = 6 * C
    touched = iota((2 * C, reach), 0) // C == (iota((2 * C, reach), 1) // C) % 2
    repeat_e = one_hot(pick_e)
    packed_x = jnp.zeros((C, reach), F32)
    packed_y = jnp.zeros((C, reach), F32)
    for tap in range(3):
        for side in range(2):
            put = one_hot(iota((C, reach), 1) == iota((C, reach), 0) + (2 * tap + side) * C)
            packed_x += dot(w1[2 * side, tap], put)
            packed_y += dot(w1[tap, 2 * side], put)
    whx[...] = jnp.where(touched, dot(repeat_e, packed_x.astype(BF16)), 0.0).astype(BF16)
    why[...] = jnp.where(touched, dot(repeat_e, packed_y.astype(BF16)), 0.0).astype(BF16)

    rows, lanes = iota((2 * 16, R), 0) % 16, iota((2 * 16, R), 1) % Y
    first = jnp.broadcast_to(fw[0:1, :].astype(F32), (16, C))
    second = jnp.broadcast_to(fw[1:2, :].astype(F32), (16, C))
    fw32 = jnp.concatenate([first, second], axis=0)
    fw16 = jnp.concatenate([first[:Y], second[:Y]], axis=0)
    highs, lows = [], []
    for i in range(3):
        for j in range(3):
            g = dot(fw32.astype(BF16), w2[i, j])
            high = g.astype(BF16)
            highs.append(high)
            lows.append((g - high.astype(F32)).astype(BF16))
    taps = dot(jnp.concatenate(highs + lows, axis=0), spread).reshape(2, 3, 3, 32, R)
    same = rows == lanes
    for part in range(2):
        for a in range(3):
            band_xy = jnp.zeros((32, R), F32)
            band_yz = jnp.zeros((32, R), F32)
            for b in range(3):
                hit = rows == (lanes + (17 - b)) % 16
                band_xy += jnp.where(hit, taps[part, b, a], 0.0)
                band_yz += jnp.where(hit, taps[part, a, b], 0.0)
            at = (part * 3 + a) * 32
            bxy[at : at + 32, :] = band_xy.astype(BF16)
            byz[at : at + 32, :] = band_yz.astype(BF16)
        for i in range(3):
            for j in range(3):
                value = jnp.where(same, taps[part, i, j], 0.0)
                at = (part * 9 + i * 3 + j) * 16
                bxz[at : at + 16, :] = jnp.concatenate([value[:Y], value[16 : 16 + Y]], axis=0).astype(BF16)
    rows, lanes = iota((R, 2 * C), 0), iota((R, 2 * C), 1)
    edge_put = one_hot(rows == (lanes % C) * Y + (lanes // C) * (Y - 1))
    bxy_e[...] = dot(bxy[...], edge_put).astype(BF16)
    byz_e[...] = dot(byz[...], edge_put).astype(BF16)
    own = iota((16, R), 0) % Y == iota((16, R), 1) % Y
    fres[...] = jnp.where(own, dot(fw16.astype(BF16), spread), 0.0).astype(BF16)
    bias = jnp.sum(fw16 * b2_row, axis=1, keepdims=True)

    peers = sum(flag.astype(jnp.int32) for flag in (*has_z, *has_y, *far))
    pl.semaphore_wait(barrier, peers)

    for side in range(2):
        @pl.when(has_z[side])
        def _():
            send_ez[side].start()
    for side in range(2):
        @pl.when(far[side])
        def _():
            for z in (*range(NEAR, K), *range(NEAR)):
                send_way[side][z].start()
            for z in range(K, Z):
                send_y[side][z].start()

        @pl.when(has_y[side] & jnp.logical_not(far[side]))
        def _():
            for z in range(Z):
                send_y[side][z].start()
    for side in range(2):
        @pl.when(has_z[side])
        def _():
            send_slab[side].start()

    def shifted(ze):
        value = ux[ze, 1].astype(F32)
        ux[ze, 0] = from_left(value).astype(BF16)
        ux[ze, 2] = from_right(value).astype(BF16)

    for ze in range(1, Z + 1):
        shifted(ze)

    row8 = iota((R, X), 0) % Y
    inner = (row8 > 0) & (row8 < Y - 1)

    def active(hidden):
        return jnp.maximum(hidden * wide(cols[2]) + wide(cols[3]), 0.0)

    def active_e(hidden):
        return jnp.maximum(hidden * wide(cols_e[0]) + wide(cols_e[1]), 0.0).astype(BF16)

    def add_xy(z, both):
        part = (both[:96] + both[96:]).reshape(3, 2, 2, Y, X)
        for j in range(3):
            acc[j, z + 1, 1] += part[j, 0]
            acc[j, z + 1, 2] += part[j, 1]

    def add_yz(z, both):
        part = (both[:96] + both[96:]).reshape(3, 2, 2, Y, X)
        for i in range(3):
            acc[1, z + 2 - i, 0] += part[i, 0]
            acc[1, z + 2 - i, 1] += part[i, 1]

    acc[...] = jnp.zeros_like(acc)
    relay(0)
    for z in range(Z):
        wide_x = ux[z + 1].reshape(3 * R, X)
        hid_e[0, z] = dot(wxy_e[...], wide_x)
        value = jnp.where(inner, active(dot(wxy[...], wide_x)), 0.0).astype(BF16)
        add_xy(z, dot(bxy[...], value))

    for side in range(2):
        @pl.when(has_z[side])
        def _():
            send_ez[side].wait_send()
            send_ez[1 - side].wait_recv()
            for yside in range(2):
                @pl.when(has_y[yside])
                def _():
                    send_corner[side][yside].start()

    relay(1)

    for z in range(Z):
        xz = dot(wxz[1], ux[z + 1].reshape(3 * R, X))
        yz = dot(wyz[1], ux[z + 1, 1])
        yz_e = dot(wyz_e[1], ux[z + 1, 1])
        for i in (0, 2):
            if 1 <= z + i <= Z:
                xz += dot(wxz[i], ux[z + i].reshape(3 * R, X))
                yz += dot(wyz[i], ux[z + i, 1])
                yz_e += dot(wyz_e[i], ux[z + i, 1])
        hid[0, z] = xz
        hid[1, z] = yz
        hid_e[1, z] = yz_e
        residual = dot(fres[...], raw[z]) + bias
        r0, r1 = residual[:Y], residual[Y:]
        acc[1, z + 1, 0, 0] += 2.0 * r0
        acc[1, z + 1, 1, 0] += r0 + r1
        acc[1, z + 1, 2, 0] += 2.0 * r1

    def finish(z):
        both = dot(bxz[...], active(hid[0, z]).astype(BF16))
        part = both[:144] + both[144:]
        for i in range(3):
            for j in range(3):
                at = (i * 3 + j) * 16
                acc[j, z + 2 - i, 0, 0] += part[at : at + Y]
                acc[j, z + 2 - i, 2, 0] += part[at + Y : at + 16]
        add_yz(z, dot(byz[...], jnp.where(inner, active(hid[1, z]), 0.0).astype(BF16)))

    for z in range(1, Z - 1):
        finish(z)

    for side in range(2):
        @pl.when(has_z[side])
        def _():
            send_slab[1 - side].wait_recv()
    for ze in (0, Z + 1):
        shifted(ze)
    for z, i in ((0, 0), (Z - 1, 2)):
        hid[0, z] += dot(wxz[i], ux[z + i].reshape(3 * R, X))
        hid[1, z] += dot(wyz[i], ux[z + i, 1])
        hid_e[1, z] += dot(wyz_e[i], ux[z + i, 1])
        finish(z)

    for side in range(2):
        @pl.when(has_y[side])
        def _():
            for z in range(Z):
                send_y[1 - side][z].wait_recv()
    hidden = []
    for z in range(Z):
        beside = halo[z + 1].reshape(2 * C, X)
        wider = beside.astype(F32)
        three = jnp.concatenate([from_left(wider).astype(BF16), beside, from_right(wider).astype(BF16)], axis=0)
        hidden.append(hid_e[0, z] + dot(whx[...], three))
    both = [dot(bxy_e[...], active_e(value)) for value in hidden]
    for z in range(Z):
        add_xy(z, both[z])
    for side in range(2):
        @pl.when(has_y[side])
        def _():
            for zside in range(2):
                @pl.when(has_z[zside])
                def _():
                    send_corner[zside][1 - side].wait_recv()
    hidden = [hid_e[1, z] + dot(why[...], halo[z : z + 3].reshape(6 * C, X)) for z in range(Z)]
    both = [dot(byz_e[...], active_e(value)) for value in hidden]
    for z in range(Z):
        add_yz(z, both[z])

    rows16x = iota((16, X), 0)
    outside = ((rows16x == 15) & jnp.logical_not(has_y[0])) | ((rows16x == Y) & jnp.logical_not(has_y[1]))
    flow = {}
    for ze in range(Z + 2):
        for comp in range(3):
            value = (
                from_left(acc[0, ze, comp].reshape(16, X))
                + acc[1, ze, comp].reshape(16, X)
                + from_right(acc[2, ze, comp].reshape(16, X))
            )
            value = jnp.where(outside, 0.0, value)
            if ze == 0:
                value = jnp.where(has_z[0], value, 0.0)
            if ze == Z + 1:
                value = jnp.where(has_z[1], value, 0.0)
            value = 0.125 * (from_left(value) + from_right(value)) + 0.25 * value
            flow[ze, comp] = 0.5 * value + 0.25 * (pltpu.roll(value, 1, axis=0) + pltpu.roll(value, 15, axis=0))
    for comp in range(3):
        for zs in range(Z + 4):
            value = None
            for ze, weight in ((zs - 2, 0.25), (zs - 1, 0.5), (zs, 0.25)):
                if 0 <= ze < Z + 2:
                    term = weight * flow[ze, comp]
                    value = term if value is None else value + term
            sm[0, zs, comp] = value[:Y]
            sm[1, zs, comp] = value[Y:]

    send_zr = [remote(zs_.at[t], zr.at[1 - t], 22 + t, z_of[t], gy) for t in range(2)]
    send_rz = [remote(sm.at[0, pl.ds((0, Z + 2)[t], 2)], rz.at[1 - t], 24 + t, z_of[t], gy) for t in range(2)]
    send_ry = [remote(ys.at[s], yr.at[1 - s], 26 + s, gz, y_of[s]) for s in range(2)]
    row = iota((Y, X), 0)
    low, high = row < 2, row >= Y - 2

    def moved(value, by):
        return pltpu.roll(value, by % Y, axis=0) if by % Y else value

    for t in range(2):
        for comp in range(3):
            a, b = sm[1, (0, Z + 2)[t], comp], sm[1, (0, Z + 2)[t] + 1, comp]
            kept = jnp.where(low, a, jnp.where(high, b, 0.0))
            zs_[t, comp] = kept + moved(jnp.where(high, a, jnp.where(low, b, 0.0)), 4)

        @pl.when(has_z[t])
        def _():
            send_zr[t].start()

    for side in range(2):
        @pl.when(jnp.logical_not(has_z[side]))
        def _():
            zr[side] = jnp.zeros((3, Y, X), F32)
            rz[side] = jnp.zeros((2, 3, Y, X), F32)

        @pl.when(jnp.logical_not(has_y[side]))
        def _():
            yr[side] = jnp.zeros((4 * Y, X), BF16)

    for side in range(2):
        @pl.when(has_z[side])
        def _():
            send_zr[1 - side].wait_recv()
    packs = [[], []]
    for comp in range(3):
        up, down = None, None
        for z in range(Z):
            value = zr[z // 2, comp]
            turned = moved(value, 4)
            if z % 2 == 0:
                value = jnp.where(low, value, turned)
            else:
                value = jnp.where(low, turned, value)
            value = sm[1, z + 2, comp] + value
            first = moved(jnp.where(low, value, 0.0), 2 * z)
            last = moved(jnp.where(high, value, 0.0), 2 * z + 2)
            up = first if up is None else up + first
            down = last if down is None else down + last
        packs[1].append(up)
        packs[0].append(down)
    for s in range(2):
        ys[s] = jnp.concatenate([*packs[s], jnp.zeros((Y, X), F32)], axis=0).astype(BF16)

        @pl.when(has_y[s])
        def _():
            send_ry[s].start()
    for t in range(2):
        @pl.when(has_z[t])
        def _():
            send_rz[t].start()

    for side in range(2):
        @pl.when(has_z[side])
        def _():
            send_rz[1 - side].wait_recv()
    for comp in range(3):
        for z in range(Z):
            sm[0, z + 2, comp] += rz[z // 2, z % 2, comp]
    for side in range(2):
        @pl.when(has_y[side])
        def _():
            send_ry[1 - side].wait_recv()
    came = [yr[s].astype(F32) for s in range(2)]
    for comp in range(3):
        for z in range(Z):
            first = moved(came[0][comp * Y : (comp + 1) * Y], -2 * z)
            last = moved(came[1][comp * Y : (comp + 1) * Y], -2 - 2 * z)
            value = jnp.where(low, first, jnp.where(high, last, 0.0))
            out[comp, z] = sm[0, z + 2, comp] + value

    for side in range(2):
        @pl.when(has_z[side])
        def _():
            send_slab[side].wait_send()
            send_zr[side].wait_send()
            send_rz[side].wait_send()

        @pl.when(far[side])
        def _():
            for z in range(K):
                send_way[side][z].wait_send()
            for z in range(K, Z):
                send_y[side][z].wait_send()

        @pl.when(has_y[side] & jnp.logical_not(far[side]))
        def _():
            for z in range(Z):
                send_y[side][z].wait_send()

        for flag, rows in ((helps[side], range(NEAR)), (near_helps[side], range(NEAR, K))):
            @pl.when(flag)
            def _():
                for z in rows:
                    pass_on[side][z].wait_send()

        @pl.when(has_y[side])
        def _():
            send_ry[side].wait_send()

        for s in range(2):
            @pl.when(has_z[side] & has_y[s])
            def _():
                send_corner[side][s].wait_send()


def block(features, s1, t1, w1, b1, s2, t2, w2, b2, fw):
    def row(v):
        return v.reshape(1, C)

    vm = pltpu.VMEM
    dma = pltpu.SemaphoreType.DMA
    return pl.pallas_call(
        kernel,
        out_shape=pltpu.VMEM((3, Z, Y, X), F32),
        in_specs=[pl.BlockSpec(memory_space=pltpu.HBM)] * 10,
        out_specs=pl.BlockSpec(memory_space=pltpu.VMEM),
        scratch_shapes=[
            vm((C, Z, Y, X), BF16),
            vm((6, 1, C), F32),
            vm((3, 3, C, C), BF16),
            vm((3, 3, C, C), BF16),
            vm((2, C), BF16),
            vm((Z, R, X), BF16),
            vm((Z + 2, 3, R, X), BF16),
            vm((Z, 2, C, X), BF16),
            vm((2, 2, C, X), BF16),
            vm((Z + 2, 2, C, X), BF16),
            vm((4, R, 128), F32),
            vm((2, 2 * C, 128), F32),
            vm((R, 3 * R), BF16),
            vm((3, R, 3 * R), BF16),
            vm((3, R, R), BF16),
            vm((2 * C, 3 * R), BF16),
            vm((3, 2 * C, R), BF16),
            vm((2 * C, 6 * C), BF16),
            vm((2 * C, 6 * C), BF16),
            vm((192, R), BF16),
            vm((288, R), BF16),
            vm((192, R), BF16),
            vm((192, 2 * C), BF16),
            vm((192, 2 * C), BF16),
            vm((16, R), BF16),
            vm((2, Z, R, X), F32),
            vm((2, Z, 2 * C, X), F32),
            vm((3, Z + 2, 3, 2, Y, X), F32),
            vm((2, Z + 4, 3, Y, X), F32),
            vm((2, Z - 1, C, X), BF16),
            vm((2, 3, Y, X), F32),
            vm((2, 3, Y, X), F32),
            vm((2, 2, 3, Y, X), F32),
            vm((2, 4 * Y, X), BF16),
            vm((2, 4 * Y, X), BF16),
            dma((Z + 9,)),
            dma((34,)),
            dma((34,)),
        ],
        compiler_params=pltpu.CompilerParams(
            collective_id=0, has_side_effects=True, vmem_limit_bytes=48 * 1024 * 1024
        ),
    )(*[pltpu.with_memory_space_constraint(v, pltpu.HBM) for v in (features, row(s1), row(t1), w1, row(b1), row(s2), row(t2), w2, row(b2), fw)])


def solution(mesh):
    return jax.shard_map(
        block,
        mesh=mesh,
        in_specs=(P(None, "gz", "gy", None), P(), P(), P(), P(), P(), P(), P(), P(), P()),
        out_specs=P(None, "gz", "gy", None),
        check_vma=False,
    )
```
